128 devices in a mesh: section: 16 (over y_lo, z, core), dp: 8 (over x, y_hi).
Axes of the slice: x: 4, y: 4 (y_hi: 2, y_lo: 2; y = y_hi * 2 + y_lo), z: 4, core: 2. Of those that a mesh axis runs over, the one named last changes fastest.
Arguments:
- anchors: bfloat16 [16, 2, 128, 16, 8192], P('section', None, 'dp'), may hold values from -6 to 6
- sample_ids: int32 [8, 8], P('dp'), may hold values from 0 to 15, as said below
- gain: float32 [16, 8192], P('section'), may hold values from 0.5 to 1.5
- w_down: bfloat16 [16, 8192, 512], P('section'), may hold values from -0.0625 to 0.0625
- w_up: bfloat16 [16, 512, 8192], P('section'), may hold values from -0.25 to 0.25
Outputs:
- new_anchors: bfloat16 [16, 128, 16, 8192], P('section', 'dp')
- grad_down: bfloat16 [16, 8192, 512], P('section', 'dp')
- grad_up: bfloat16 [16, 512, 8192], P('section', None, 'dp')
The draws below stay inside these ranges and needn't reach their ends.
Inputs may be any that keep to these rules, and one draw needn't show every extreme that they name: `sample_ids`: the 8 entries of a row are distinct slots of that replica's 16 stored samples.
All inputs are finite; a program needn't handle non-finite values. Where the reference program divides by a largest or mean magnitude, that divisor is 1e-20 or more.
Results may differ from the reference program's by a relative error of at most 0.04.
Values may be sent and summed in bfloat16 or wider, within the bound.
No kernel may reach another device: no remote copies, remote signals or barrier semaphores. Data moves between devices by JAX's collectives and lax.ppermute only.
A program may use at most 192 MiB of HBM per device.

```python
import jax
import jax.numpy as jnp
from jax import lax

D = 8192
R = 512
MICRO = 8
SEQ = 16
STORE = 16
SLOTS = 128
N_SECTION = 16
N_DP = 8


def draw_sample_ids(key, part):
    key = jax.random.fold_in(key, 11)

    def one_row(row):
        row_key = jax.random.fold_in(key, row)
        first_key, second_key = jax.random.split(row_key)
        chosen = jax.random.permutation(first_key, STORE - 1)[:MICRO - 1].astype(jnp.int32)
        full = jnp.concatenate([chosen, jnp.full((1,), STORE - 1, jnp.int32)])
        order = jax.random.permutation(second_key, MICRO)
        return full[order].astype(jnp.int32)
    return jax.vmap(one_row)(jnp.arange(N_DP, dtype=jnp.int32))


def block_scale(stream_key, shape, cuts, least, high):
    level, own = 1.0, jax.random.fold_in(stream_key, 6)
    for position, shards_of in cuts:
        steps = jnp.exp(jax.random.uniform(jax.random.fold_in(own, position), (shards_of,), jnp.float32, least / len(cuts), high / len(cuts)))
        level = level * jnp.repeat(steps, shape[position] // shards_of).reshape([-1 if axis == position else 1 for axis in range(len(shape))])
    return level


def bell_draw(rng, dims, deviation, bound, cuts=(), kind=jnp.bfloat16):
    array = jax.random.normal(rng, dims, jnp.float32) * deviation
    if len(cuts) > 0:
        array = block_scale(rng, dims, cuts, -0.22, 0.18) * array
    return jnp.clip(array, min=-bound, max=bound).astype(kind)


def setup_inputs(seed: int = 0) -> dict:
    splits = jax.random.split(jax.random.key(seed), 6)
    anchors = bell_draw(splits[0], (N_SECTION, 2, SLOTS, SEQ, D), 1.0, 6.0, ((0, 16), (2, 8)))
    sample_ids = draw_sample_ids(jax.random.fold_in(splits[5], 71), 0)
    gain = jnp.clip(1.0 + 0.1 * jax.random.normal(splits[2], (N_SECTION, D), jnp.float32), 0.5, 1.5)
    w_down = bell_draw(splits[3], (N_SECTION, D, R), D ** -0.5, 0.0625, ((0, 16),))
    w_up = bell_draw(splits[4], (N_SECTION, R, D), R ** -0.5, 0.25, ((0, 16),))
    return dict(anchors=anchors, sample_ids=sample_ids, gain=gain, w_down=w_down, w_up=w_up)


def layer(entry, gains, w_a, w_b):
    h = entry.astype(jnp.float32)
    r = lax.rsqrt(lax.optimization_barrier(jnp.mean(h * h, -1, keepdims=True)) + 1e-05)
    normed = (h * r * gains).astype(jnp.bfloat16)
    z = jnp.dot(normed, w_a, preferred_element_type=jnp.float32)
    acted = jax.nn.silu(z).astype(jnp.bfloat16)
    result = (h + jnp.dot(acted, w_b, preferred_element_type=jnp.float32)).astype(jnp.bfloat16)
    return (h, r, normed, z, acted, result)

def layer_back(h, r, z, dy, gains, w_a, w_b):
    dyb = dy.astype(jnp.bfloat16)
    dg = jnp.dot(dyb, w_b.T, preferred_element_type=jnp.float32)
    sig = jax.nn.sigmoid(z)
    dzb = (dg * sig * (1.0 + z * (1.0 - sig))).astype(jnp.bfloat16)
    da = jnp.dot(dzb, w_a.T, preferred_element_type=jnp.float32)
    u = da * gains
    dh = r * u - h * (r * r * r) * lax.optimization_barrier(jnp.mean(h * u, -1, keepdims=True))
    return (dyb, dzb, dy + dh)

def quantize(grad):
    rows, width = grad.shape
    blocks = grad.reshape(rows, width // 128, 128)
    scales = (lax.optimization_barrier(jnp.max(jnp.abs(blocks), -1)) + 1e-06).astype(jnp.bfloat16)
    levels = (blocks / scales.astype(jnp.float32)[..., None]).astype(jnp.bfloat16)
    return (levels.reshape(rows, width), scales)

def dequantize(levels, scales):
    rows, width = levels.shape
    blocks = levels.astype(jnp.float32).reshape(rows, width // 128, 128)
    return (blocks * scales.astype(jnp.float32)[..., None]).reshape(rows, width)

def reference(anchors, sample_ids, gain, w_down, w_up):
    sections = anchors.shape[0]
    replicas, micro = sample_ids.shape
    width = anchors.shape[-1]
    per_replica = anchors.shape[2] // replicas
    offsets = per_replica * jnp.arange(replicas, dtype=jnp.int32)[:, None]
    slots = (sample_ids + offsets).reshape(-1).astype(jnp.int32)

    def pick(block):
        return jnp.take(block, slots, axis=0).reshape(-1, width)
    inputs = []
    stored = []
    entry = pick(anchors[0, 0])
    result = entry
    for s in range(sections):
        if s > 0:
            delta = (result.astype(jnp.float32) - pick(anchors[s - 1, 1]).astype(jnp.float32)).astype(jnp.bfloat16)
            entry = (pick(anchors[s, 0]).astype(jnp.float32) + delta.astype(jnp.float32)).astype(jnp.bfloat16)
        inputs.append(entry)
        stored.append(anchors[s, 0].at[slots].set(entry.reshape(-1, SEQ, width)))
        result = layer(entry, gain[s], w_down[s], w_up[s])[5]
    grads_down = [None] * sections
    grads_up = [None] * sections
    back = None
    for s in range(sections - 1, -1, -1):
        h, r, normed, z, acted, result = layer(inputs[s], gain[s], w_down[s], w_up[s])
        if s == sections - 1:
            dy = result.astype(jnp.float32) - pick(anchors[s, 1]).astype(jnp.float32)
        else:
            dy = dequantize(*quantize(back))
        dyb, dzb, back = layer_back(h, r, z, dy, gain[s], w_down[s], w_up[s])
        grads_down[s] = jnp.dot(normed.T, dzb, preferred_element_type=jnp.float32).astype(jnp.bfloat16)
        grads_up[s] = jnp.dot(acted.T, dyb, preferred_element_type=jnp.float32).astype(jnp.bfloat16)
    return (jnp.stack(stored), jnp.stack(grads_down), jnp.stack(grads_up))
```

```python
import jax
import jax.numpy as jnp
from jax import lax
from jax.experimental import pallas as pl
from jax.experimental.pallas import tpu as pltpu
from jax.sharding import PartitionSpec as P

bf16 = jnp.bfloat16
f32 = jnp.float32
VMEM = pltpu.VMEM
PARAMS = pltpu.CompilerParams(vmem_limit_bytes=8 * 2 ** 20)
TASKS = 16


def vmem_spec():
    return pl.BlockSpec(memory_space=VMEM)


def smem_spec():
    return pl.BlockSpec(memory_space=pltpu.SMEM)


def hbm_spec():
    return pl.BlockSpec(memory_space=pltpu.HBM)


def in_vmem(x):
    return pltpu.with_memory_space_constraint(x, VMEM)


def nn(a, w):
    return lax.dot_general(a, w, (((1,), (0,)), ((), ())), preferred_element_type=f32)


def sigmoid(z):
    return 1.0 / (1.0 + jnp.exp(-z))


def idle_task(t, start, micro):
    return jnp.where(t < start, t, t - micro)


def load_kernel(slots, anchors, gain, w_down, w_up, base, sent, gv, wd, wu, sems):
    micro = base.shape[0]
    copies = [
        pltpu.make_async_copy(w_down.at[0], wd, sems.at[0]),
        pltpu.make_async_copy(w_up.at[0], wu, sems.at[1]),
        pltpu.make_async_copy(gain, gv, sems.at[2]),
    ]
    for m in range(micro):
        copies.append(pltpu.make_async_copy(anchors.at[0, 0, slots[m]], base.at[m], sems.at[3 + m]))
        copies.append(pltpu.make_async_copy(anchors.at[0, 1, slots[m]], sent.at[m], sems.at[3 + micro + m]))
    for c in copies:
        c.start()
    for c in copies:
        c.wait()


def load(slots, anchors, gain, w_down, w_up):
    micro = slots.shape[0]
    seq, width = anchors.shape[3:]
    rank = w_down.shape[2]
    return pl.pallas_call(
        load_kernel,
        name="load",
        compiler_params=PARAMS,
        out_shape=[
            VMEM((micro, seq, width), bf16),
            VMEM((micro, seq, width), bf16),
            VMEM((1, width), f32),
            VMEM((width, rank), bf16),
            VMEM((rank, width), bf16),
        ],
        in_specs=[smem_spec()] + [hbm_spec()] * 4,
        out_specs=[vmem_spec()] * 5,
        scratch_shapes=[pltpu.SemaphoreType.DMA((3 + 2 * micro,))],
    )(slots, anchors, gain, w_down, w_up)


def forward_kernel(t, last, place, delta_in, base, sent, gain, wd, wu,
                   x_old, z_old, r_old, ag_old, dyz_old, wdt_old, wut_old,
                   delta_out, x_all, z_all, r_all, ag, dyz, wdt, wut):
    s = place[0]
    m = t - 2 * s
    micro, seq, width = base.shape
    rank = wd.shape[1]
    share = width // ag.shape[0]
    cols = [(d, slice(d * share, (d + 1) * share)) for d in range(ag.shape[0])]
    busy = (m >= 0) & (m < micro)
    task = idle_task(t, 2 * s, micro)

    @pl.when(jnp.logical_not(busy) & (task < TASKS))
    def _():
        step = width // TASKS
        part = pl.ds(pl.multiple_of(task * step, step), step)
        wut[part, :] = wu[:, part].T
        wdt[:, part] = wd[part, :].T

    @pl.when(busy)
    def _():
        total = jnp.zeros((seq, 128), f32)
        for d, c in cols:
            x = (base[m, :, c].astype(f32) + delta_in[:, c].astype(f32)).astype(bf16)
            x_all[m, :, c] = x
            h = x.astype(f32)
            sq = h * h
            for k in range(0, share, 128):
                total = total + sq[:, k:k + 128]
        r = lax.rsqrt(jnp.sum(total, -1, keepdims=True) / width + 1e-05)
        r_all[m] = jnp.broadcast_to(r, (seq, 128))
        z = None
        for d, c in cols:
            a = (x_all[m, :, c].astype(f32) * r * gain[:, c]).astype(bf16)
            ag[d, m, :, :share] = a
            part = nn(a, wd[c, :])
            z = part if z is None else z + part
        z_all[m] = z
        g = (z * sigmoid(z)).astype(bf16)
        for d, c in cols:
            ag[d, m, :, share:] = g
            y = (x_all[m, :, c].astype(f32) + nn(g, wu[:, c])).astype(bf16)
            delta_out[:, c] = (y.astype(f32) - sent[m, :, c].astype(f32)).astype(bf16)

        @pl.when(s == last)
        def _():
            for d, c in cols:
                dyz[d, m, :, :share] = delta_out[:, c]


def forward_step(t, last, place, delta, base, sent, gain, wd, wu, state):
    micro, seq, width = base.shape
    rank = wd.shape[1]
    out = pl.pallas_call(
        lambda *refs: forward_kernel(t, last, *refs),
        name="forward",
        compiler_params=PARAMS,
        out_shape=[jax.ShapeDtypeStruct((seq, width), bf16)] + [VMEM(v.shape, v.dtype) for v in state],
        in_specs=[smem_spec()] + [vmem_spec()] * (6 + len(state)),
        out_specs=[vmem_spec()] * (1 + len(state)),
        input_output_aliases={7 + i: 1 + i for i in range(len(state))},
        cost_estimate=pl.CostEstimate(flops=4 * seq * width * rank, bytes_accessed=2 ** 20, transcendentals=0),
    )(place, delta, *[in_vmem(v) for v in (base, sent, gain, wd, wu, *state)])
    return out[0], out[1:]


def backward_kernel(t, last, place, owner, dy_in, gain, wdt, wut, x_all, z_all, r_all, anchors,
                    dyz_old, kept_old, dx_out, dyz, kept, sems):
    s = place[0]
    m = t - 2 * (last - s)
    micro, seq, width = x_all.shape
    share = width // dyz.shape[0]
    cols = [(d, slice(d * share, (d + 1) * share)) for d in range(dyz.shape[0])]
    busy = (m >= 0) & (m < micro)
    task = idle_task(t, 2 * (last - s), micro)

    @pl.when(jnp.logical_not(busy) & (task < kept.shape[1]))
    def _():
        @pl.when(owner[task] >= 0)
        def _():
            copy = pltpu.make_async_copy(x_all.at[owner[task]], kept.at[0, task], sems.at[0])
            copy.start()
            copy.wait()

        @pl.when(owner[task] < 0)
        def _():
            copy = pltpu.make_async_copy(anchors.at[0, 0, task], kept.at[0, task], sems.at[0])
            copy.start()
            copy.wait()

    @pl.when(busy)
    def _():
        @pl.when(s < last)
        def _():
            for d, c in cols:
                dyz[d, m, :, :share] = dy_in[:, c]

        dg = None
        for d, c in cols:
            part = nn(dyz[d, m, :, :share], wut[c, :])
            dg = part if dg is None else dg + part
        z = z_all[m]
        sig = sigmoid(z)
        dz = (dg * sig * (1.0 + z * (1.0 - sig))).astype(bf16)
        for d, c in cols:
            dyz[d, m, :, share:] = dz

        @pl.when(s > 0)
        def _():
            r = r_all[m][:, :1]
            coef = r * r * (jnp.sum(dz.astype(f32) * z, -1, keepdims=True) / width)
            for d, c in cols:
                u = nn(dz, wdt[:, c]) * gain[:, c]
                dx = dyz[d, m, :, :share].astype(f32) + r * u - x_all[m, :, c].astype(f32) * coef
                dx_out[:, c] = dx.astype(bf16)


def backward_step(t, last, place, owner, dy, gain, wdt, wut, x_all, z_all, r_all, anchors, dyz, kept):
    micro, seq, width = x_all.shape
    rank = wdt.shape[0]
    return pl.pallas_call(
        lambda *refs: backward_kernel(t, last, *refs),
        name="backward",
        compiler_params=PARAMS,
        out_shape=[
            jax.ShapeDtypeStruct((seq, width), bf16),
            VMEM(dyz.shape, bf16),
            jax.ShapeDtypeStruct(kept.shape, bf16),
        ],
        in_specs=[smem_spec()] * 2 + [vmem_spec()] * 7 + [hbm_spec(), vmem_spec(), hbm_spec()],
        out_specs=[vmem_spec(), vmem_spec(), hbm_spec()],
        input_output_aliases={10: 1, 11: 2},
        scratch_shapes=[pltpu.SemaphoreType.DMA((1,))],
        cost_estimate=pl.CostEstimate(flops=4 * seq * width * rank, bytes_accessed=2 ** 20, transcendentals=0),
    )(place, owner, dy, *[in_vmem(v) for v in (gain, wdt, wut, x_all, z_all, r_all)], anchors, in_vmem(dyz), kept)


def empty(shape, dtype):
    return pl.pallas_call(
        lambda o: None, name="empty", compiler_params=PARAMS, out_shape=VMEM(shape, dtype), out_specs=vmem_spec()
    )()


def empty_hbm(shape, dtype):
    return pl.pallas_call(
        lambda o: None, name="empty", compiler_params=PARAMS, out_shape=jax.ShapeDtypeStruct(shape, dtype),
        out_specs=hbm_spec()
    )()


def shards(anchors, sample_ids, gain, w_down, w_up):
    section = lax.axis_index("section")
    sections = lax.axis_size("section")
    replicas = lax.axis_size("dp")
    slots = sample_ids[0]
    micro = slots.shape[0]
    store, seq, width = anchors.shape[2:]
    rank = w_down.shape[2]
    last = sections - 1
    steps = micro + 2 * last
    rows = micro * seq
    share = width // replicas
    place = jnp.full((1,), section, jnp.int32)
    pairs = micro // 2

    def hops(t):
        final = (steps - 1) // 2 - 2
        k = t // 2
        low = 0 if k < 3 else min((k - 1) // 2 * 2 + 1, final - 2)
        high = low + 2 if low == 0 or low + 2 >= final else low + 1
        return [s for s in range(max(0, low - pairs + 1), min(last - 1, high) + 1)]

    base, sent, gv, wd, wu = load(slots, anchors, gain, w_down, w_up)
    state = [
        empty((micro, seq, width), bf16),
        empty((micro, seq, rank), f32),
        empty((micro, seq, 128), f32),
        empty((replicas, micro, seq, share + rank), bf16),
        empty((replicas, micro, seq, share + rank), bf16),
        empty((rank, width), bf16),
        empty((width, rank), bf16),
    ]
    nothing = jnp.zeros((seq, width), bf16)
    arrived = [nothing, nothing]
    for t in range(steps):
        delta, state = forward_step(t, last, place, arrived[t], base, sent, gv, wd, wu, state)
        if t < steps - 2:
            arrived.append(lax.ppermute(delta, "section", [(s, s + 1) for s in hops(t)]))
    x_all, z_all, r_all, ag, dyz, wdt, wut = state
    ag = lax.all_to_all(ag, "dp", 0, 0, tiled=True).reshape(replicas * rows, share + rank)

    match = slots[None, :] == jnp.arange(store, dtype=jnp.int32)[:, None]
    owner = jnp.max(jnp.where(match, jnp.arange(micro, dtype=jnp.int32)[None, :], -1), 1).astype(jnp.int32)
    kept = empty_hbm((1, store, seq, width), bf16)
    arrived = [nothing, nothing]
    for t in range(steps):
        dx, dyz, kept = backward_step(
            t, last, place, owner, arrived[t], gv, wdt, wut, x_all, z_all, r_all, anchors, dyz, kept)
        if t < steps - 2:
            arrived.append(lax.ppermute(dx, "section", [(last - s, last - s - 1) for s in hops(t)]))

    dyz = lax.all_to_all(dyz, "dp", 0, 0, tiled=True).reshape(replicas * rows, share + rank)
    grad_down = jnp.dot(ag[:, :share].T, dyz[:, share:], preferred_element_type=f32).astype(bf16)
    grad_up = jnp.dot(ag[:, share:].T, dyz[:, :share], preferred_element_type=f32).astype(bf16)
    return kept, grad_down[None], grad_up[None]


def solution(mesh):
    placed = (
        P("section", None, "dp", None, None),
        P("dp", None),
        P("section", None),
        P("section", None, None),
        P("section", None, None),
    )
    return jax.shard_map(
        shards,
        mesh=mesh,
        in_specs=placed,
        out_specs=(
            P("section", "dp", None, None),
            P("section", "dp", None),
            P("section", None, "dp"),
        ),
        check_vma=False,
    )
```

```python
import jax
import jax.numpy as jnp
from jax import lax
from jax.experimental import pallas as pl
from jax.experimental.pallas import tpu as pltpu
from jax.sharding import PartitionSpec as P

bf16 = jnp.bfloat16
f32 = jnp.float32
VMEM = pltpu.VMEM
PARAMS = pltpu.CompilerParams(vmem_limit_bytes=8 * 2 ** 20)
TASKS = 16


def vmem_spec():
    return pl.BlockSpec(memory_space=VMEM)


def smem_spec():
    return pl.BlockSpec(memory_space=pltpu.SMEM)


def hbm_spec():
    return pl.BlockSpec(memory_space=pltpu.HBM)


def in_vmem(x):
    return pltpu.with_memory_space_constraint(x, VMEM)


def in_hbm(x):
    return pltpu.with_memory_space_constraint(x, pltpu.HBM)


def nn(a, w):
    return lax.dot_general(a, w, (((1,), (0,)), ((), ())), preferred_element_type=f32)


def sigmoid(z):
    return 1.0 / (1.0 + jnp.exp(-z))


def idle_task(t, start, micro):
    return jnp.where(t < start, t, t - micro)


def load_kernel(section, replica, slots, anchors, gain, w_down, w_up, base, sent, gv, wd, wu, *rest):
    sems = rest[-1]
    micro = base.shape[0]
    copies = [
        pltpu.make_async_copy(w_down.at[0], wd, sems.at[0]),
        pltpu.make_async_copy(w_up.at[0], wu, sems.at[1]),
        pltpu.make_async_copy(gain, gv, sems.at[2]),
    ]
    for m in range(micro):
        copies.append(pltpu.make_async_copy(anchors.at[0, 0, slots[m]], base.at[m], sems.at[3 + m]))
        copies.append(pltpu.make_async_copy(anchors.at[0, 1, slots[m]], sent.at[m], sems.at[3 + micro + m]))
    for c in copies:
        c.start()
    for c in copies:
        c.wait()


def load(section, replica, slots, anchors, gain, w_down, w_up, state):
    micro = slots.shape[0]
    seq, width = anchors.shape[3:]
    rank = w_down.shape[2]
    shapes = [
        VMEM((micro, seq, width), bf16),
        VMEM((micro, seq, width), bf16),
        VMEM((1, width), f32),
        VMEM((width, rank), bf16),
        VMEM((rank, width), bf16),
    ] + [VMEM(shape, dtype) for shape, dtype in state]
    out = pl.pallas_call(
        load_kernel,
        name="load",
        compiler_params=PARAMS,
        out_shape=shapes,
        in_specs=[smem_spec()] * 3 + [hbm_spec()] * 4,
        out_specs=[vmem_spec()] * len(shapes),
        scratch_shapes=[pltpu.SemaphoreType.DMA((3 + 2 * micro,))],
    )(section, replica, slots, *[in_hbm(v) for v in (anchors, gain, w_down, w_up)])
    return out[:5], out[5:]


def forward_kernel(t, last, section, delta_in, base, sent, gain, wd, wu,
                   x_old, z_old, r_old, a_old, g_old, dyz_old, wdt_old, wut_old,
                   delta_out, x_all, z_all, r_all, a_all, g_all, dyz, wdt, wut):
    s = section[0]
    m = t - 2 * s
    micro, seq, width = base.shape
    rank = wd.shape[1]
    share = width // dyz.shape[0]
    cols = [(d, slice(d * share, (d + 1) * share)) for d in range(dyz.shape[0])]
    busy = (m >= 0) & (m < micro)
    task = idle_task(t, 2 * s, micro)

    @pl.when(jnp.logical_not(busy) & (task < TASKS))
    def _():
        step = width // TASKS
        part = pl.ds(pl.multiple_of(task * step, step), step)
        wut[part, :] = wu[:, part].T
        wdt[:, part] = wd[part, :].T

    @pl.when(busy)
    def _():
        total = jnp.zeros((seq, 128), f32)
        for d, c in cols:
            x = (base[m, :, c].astype(f32) + delta_in[:, c].astype(f32)).astype(bf16)
            x_all[m, :, c] = x
            h = x.astype(f32)
            sq = h * h
            for k in range(0, share, 128):
                total = total + sq[:, k:k + 128]
        r = lax.rsqrt(jnp.sum(total, -1, keepdims=True) / width + 1e-05)
        r_all[m] = jnp.broadcast_to(r, (seq, 128))
        z = None
        for d, c in cols:
            a = (x_all[m, :, c].astype(f32) * r * gain[:, c]).astype(bf16)
            a_all[m, :, c] = a
            part = nn(a, wd[c, :])
            z = part if z is None else z + part
        z_all[m] = z
        g = (z * sigmoid(z)).astype(bf16)
        g_all[m] = g
        for d, c in cols:
            y = (x_all[m, :, c].astype(f32) + nn(g, wu[:, c])).astype(bf16)
            delta_out[:, c] = (y.astype(f32) - sent[m, :, c].astype(f32)).astype(bf16)

        @pl.when(s == last)
        def _():
            for d, c in cols:
                dyz[d, m, :, :share] = delta_out[:, c]


def forward_step(t, last, section, delta, base, sent, gain, wd, wu, state):
    micro, seq, width = base.shape
    rank = wd.shape[1]
    out = pl.pallas_call(
        lambda *refs: forward_kernel(t, last, *refs),
        name="forward",
        compiler_params=PARAMS,
        out_shape=[jax.ShapeDtypeStruct((seq, width), bf16)] + [VMEM(v.shape, v.dtype) for v in state],
        in_specs=[smem_spec()] + [vmem_spec()] * (6 + len(state)),
        out_specs=[vmem_spec()] * (1 + len(state)),
        input_output_aliases={7 + i: 1 + i for i in range(len(state))},
        cost_estimate=pl.CostEstimate(flops=4 * seq * width * rank, bytes_accessed=2 ** 20, transcendentals=0),
    )(section, delta, *[in_vmem(v) for v in (base, sent, gain, wd, wu, *state)])
    return out[0], out[1:]


def of_section(values, s):
    found = jnp.int32(0)
    for i, v in enumerate(values):
        if v:
            found = jnp.where(s == i, jnp.int32(v), found)
    return found


def backward_kernel(t, last, kinds, section, replica, dy_in, gain, wdt, wut, x_all, z_all, r_all, a_all, g_all,
                    dyz_old, at_old, gt_old, dx_out, dyz, at, gt):
    s, q = section[0], replica[0]
    m = t - 2 * (last - s)
    micro, seq, width = x_all.shape
    rank = wdt.shape[0]
    replicas = dyz.shape[0]
    share = width // replicas
    rows = micro * seq
    cols = [(d, slice(d * share, (d + 1) * share)) for d in range(replicas)]
    busy = (m >= 0) & (m < micro)

    def share_of(d):
        return pl.ds(pl.multiple_of(d * share, share), share)

    def rows_of(d):
        return pl.ds(pl.multiple_of(d * rows, rows), rows)

    if t >= 2 and any(kinds[t - 2]):
        came = of_section(kinds[t - 2], s)
        source = lax.rem(q + replicas - came // 4, replicas)

        @pl.when(came % 4 == 1)
        def _():
            block = jnp.concatenate([dy_in[:, i * share:(i + 1) * share] for i in range(micro)], 0)
            at[:, rows_of(source)] = block.T

        @pl.when(came % 4 == 2)
        def _():
            block = jnp.concatenate([dy_in[:, i * rank:(i + 1) * rank] for i in range(micro)], 0)
            gt[:, rows_of(source)] = block.T

    if any(kinds[t]):
        goes = of_section(kinds[t], s)
        target = lax.rem(q + goes // 4, replicas)

        @pl.when(goes % 4 == 1)
        def _():
            for i in range(micro):
                dx_out[:, i * share:(i + 1) * share] = a_all[i, :, share_of(target)]

        @pl.when(goes % 4 == 2)
        def _():
            for i in range(micro):
                dx_out[:, i * rank:(i + 1) * rank] = g_all[i]

        if any(v == 3 for v in kinds[t]):
            @pl.when(goes == 3)
            def _():
                at[:, rows_of(q)] = jnp.concatenate([a_all[i, :, share_of(q)] for i in range(micro)], 0).T
                gt[:, rows_of(q)] = jnp.concatenate([g_all[i] for i in range(micro)], 0).T

    @pl.when(busy)
    def _():
        dg = None
        for d, c in cols:
            dy = dy_in[:, c]
            if t < micro:
                dy = jnp.where(s == last, dyz[d, m, :, :share], dy)
            dyz[d, m, :, :share] = dy
            part = nn(dy, wut[c, :])
            dg = part if dg is None else dg + part
        z = z_all[m]
        sig = sigmoid(z)
        dz = (dg * sig * (1.0 + z * (1.0 - sig))).astype(bf16)
        for d, c in cols:
            dyz[d, m, :, share:] = dz

        @pl.when(s > 0)
        def _():
            r = r_all[m][:, :1]
            coef = r * r * (jnp.sum(dz.astype(f32) * z, -1, keepdims=True) / width)
            for d, c in cols:
                u = nn(dz, wdt[:, c]) * gain[:, c]
                dx = dyz[d, m, :, :share].astype(f32) + r * u - x_all[m, :, c].astype(f32) * coef
                dx_out[:, c] = dx.astype(bf16)


def backward_step(t, last, kinds, section, replica, dy, fixed, state):
    gain, wdt, wut, x_all = fixed[:4]
    micro, seq, width = x_all.shape
    rank = wdt.shape[0]
    out = pl.pallas_call(
        lambda *refs: backward_kernel(t, last, kinds, *refs),
        name="backward",
        compiler_params=PARAMS,
        out_shape=[jax.ShapeDtypeStruct((seq, width), bf16)] + [VMEM(v.shape, v.dtype) for v in state],
        in_specs=[smem_spec()] * 2 + [vmem_spec()] * 12,
        out_specs=[vmem_spec()] * 4,
        input_output_aliases={11: 1, 12: 2, 13: 3},
        cost_estimate=pl.CostEstimate(flops=4 * seq * width * rank, bytes_accessed=2 ** 20, transcendentals=0),
    )(section, replica, dy, *[in_vmem(v) for v in fixed], *[in_vmem(v) for v in state])
    return out[0], out[1:]


def keep_kernel(owner, anchors, x_all, kept, sems):
    slots = kept.shape[1]
    for j in range(slots):
        @pl.when(owner[j] >= 0)
        def _():
            pltpu.make_async_copy(x_all.at[owner[j]], kept.at[0, j], sems.at[j]).start()

        @pl.when(owner[j] < 0)
        def _():
            pltpu.make_async_copy(anchors.at[0, 0, j], kept.at[0, j], sems.at[j]).start()
    for j in range(slots):
        pltpu.make_async_copy(anchors.at[0, 0, j], kept.at[0, j], sems.at[j]).wait()


def keep(owner, anchors, x_all):
    shape = (1, *anchors.shape[2:])
    return pl.pallas_call(
        keep_kernel,
        name="keep",
        compiler_params=PARAMS,
        out_shape=pltpu.HBM(shape, bf16),
        in_specs=[smem_spec(), hbm_spec(), hbm_spec()],
        out_specs=hbm_spec(),
        scratch_shapes=[pltpu.SemaphoreType.DMA((shape[1],))],
    )(owner, in_hbm(anchors), in_hbm(x_all))


def pack_kernel(dyz, out, sem):
    copy = pltpu.make_async_copy(dyz, out, sem)
    copy.start()
    copy.wait()


def pack(dyz):
    return pl.pallas_call(
        pack_kernel,
        name="pack",
        compiler_params=PARAMS,
        out_shape=pltpu.HBM(dyz.shape, bf16),
        in_specs=[vmem_spec()],
        out_specs=hbm_spec(),
        scratch_shapes=[pltpu.SemaphoreType.DMA],
    )(in_vmem(dyz))


def gradients_kernel(at, gt, dyz, down, up):
    share = at.shape[0]
    rank = gt.shape[0]
    block = 512

    def down_rows(i, _):
        part = pl.ds(pl.multiple_of(i * block, block), block)
        down[part, :] = nn(at[part, :], dyz[:, share:]).astype(bf16)
        return 0

    def up_rows(i, _):
        part = pl.ds(pl.multiple_of(i * block, block), block)
        up[part, :] = nn(gt[part, :], dyz[:, :share]).astype(bf16)
        return 0

    lax.fori_loop(0, share // block, down_rows, 0)
    lax.fori_loop(0, rank // block, up_rows, 0)


def gradients(at, gt, dyz):
    share, rows = at.shape
    rank = gt.shape[0]
    return pl.pallas_call(
        gradients_kernel,
        name="gradients",
        compiler_params=pltpu.CompilerParams(vmem_limit_bytes=24 * 2 ** 20),
        out_shape=[jax.ShapeDtypeStruct((share, rank), bf16), jax.ShapeDtypeStruct((rank, share), bf16)],
        in_specs=[vmem_spec()] * 3,
        out_specs=[vmem_spec()] * 2,
    )(in_vmem(at), in_vmem(gt), dyz)


def empty(shapes):
    return pl.pallas_call(
        lambda *o: None, name="empty", compiler_params=PARAMS, out_shape=[VMEM(*v) for v in shapes],
        out_specs=[vmem_spec()] * len(shapes)
    )()


def hops(t, last, steps, micro):
    final = (steps - 1) // 2 - 2
    k = t // 2
    low = 0 if k < 3 else min((k - 1) // 2 * 2 + 1, final - 2)
    high = low + 2 if low == 0 or low + 2 >= final else low + 1
    return low, [s for s in range(max(0, low - micro // 2 + 1), min(last - 1, high) + 1)]


def ride(last, steps, micro, replicas):
    sent = [{} for _ in range(last + 1)]
    pairs, kinds = [], []
    for t in range(steps):
        kind = [0] * (last + 1)
        perm = []
        if t < steps - 2:
            low, senders = hops(t, last, steps, micro)
            taken = {last - s for s in senders} | {last - s - 1 for s in senders}
            for s in senders:
                perm += [((last - s) * replicas + q, (last - s - 1) * replicas + q) for q in range(replicas)]
            for s in range(last + 1):
                if s in taken:
                    continue
                slot = (low, t % 2)
                if slot not in sent[s] and len(sent[s]) < replicas - 1:
                    sent[s][slot] = [len(sent[s]) + 1, 0]
                if slot in sent[s]:
                    distance, count = sent[s][slot]
                    perm += [(s * replicas + q, s * replicas + (q + distance) % replicas) for q in range(replicas)]
                    if count < 2:
                        kind[s] = 4 * distance + count + 1
                        sent[s][slot][1] += 1
        pairs.append(perm)
        kinds.append(kind)
    for s in range(last + 1):
        assert sorted(v[0] for v in sent[s].values()) == list(range(1, replicas))
        assert all(v[1] == 2 for v in sent[s].values())
        free = [t for t in range(steps) if kinds[t][s] == 0 and not 0 <= t - 2 * (last - s) < micro]
        kinds[free[-1]][s] = 3
    return pairs, kinds


def shards(anchors, sample_ids, gain, w_down, w_up):
    section = jnp.full((1,), lax.axis_index("section"), jnp.int32)
    replica = jnp.full((1,), lax.axis_index("dp"), jnp.int32)
    sections = lax.axis_size("section")
    replicas = lax.axis_size("dp")
    slots = sample_ids[0]
    micro = slots.shape[0]
    store, seq, width = anchors.shape[2:]
    rank = w_down.shape[2]
    last = sections - 1
    steps = micro + 2 * last
    rows = micro * seq
    share = width // replicas
    pairs, kinds = ride(last, steps, micro, replicas)
    match = slots[None, :] == jnp.arange(store, dtype=jnp.int32)[:, None]
    owner = jnp.max(jnp.where(match, jnp.arange(micro, dtype=jnp.int32)[None, :], -1), 1).astype(jnp.int32)
    nothing = jnp.zeros((seq, width), bf16)
    slots, owner, nothing = lax.optimization_barrier((slots, owner, nothing))

    (base, sent, gv, wd, wu), state = load(section, replica, slots, anchors, gain, w_down, w_up, [
        ((micro, seq, width), bf16),
        ((micro, seq, rank), f32),
        ((micro, seq, 128), f32),
        ((micro, seq, width), bf16),
        ((micro, seq, rank), bf16),
        ((replicas, micro, seq, share + rank), bf16),
        ((rank, width), bf16),
        ((width, rank), bf16),
    ])
    arrived = [nothing, nothing]
    for t in range(steps):
        delta, state = forward_step(t, last, section, arrived[t], base, sent, gv, wd, wu, state)
        if t < steps - 2:
            senders = hops(t, last, steps, micro)[1]
            arrived.append(lax.ppermute(delta, "section", [(s, s + 1) for s in senders]))
    x_all, z_all, r_all, a_all, g_all, dyz, wdt, wut = state

    state = [dyz, *empty([((share, replicas * rows), bf16), ((rank, replicas * rows), bf16)])]
    fixed = [gv, wdt, wut, x_all, z_all, r_all, a_all, g_all]
    arrived = [nothing, nothing]
    for t in range(steps):
        dx, state = backward_step(t, last, kinds, section, replica, arrived[t], fixed, state)
        if t < steps - 2:
            arrived.append(lax.ppermute(dx, ("section", "dp"), pairs[t]))
    dyz, at, gt = state
    dyz, x_all = lax.optimization_barrier((pack(dyz), x_all))
    kept = keep(owner, anchors, x_all)
    dyz = lax.all_to_all(dyz, "dp", 0, 0, tiled=True).reshape(replicas * rows, share + rank)
    grad_down, grad_up = gradients(at, gt, dyz)
    return kept, grad_down[None], grad_up[None]


def solution(mesh):
    placed = (
        P("section", None, "dp", None, None),
        P("dp", None),
        P("section", None),
        P("section", None, None),
        P("section", None, None),
    )
    return jax.shard_map(
        shards,
        mesh=mesh,
        in_specs=placed,
        out_specs=(
            P("section", "dp", None, None),
            P("section", "dp", None),
            P("section", None, "dp"),
        ),
        check_vma=False,
    )
```

```python
import jax
import jax.numpy as jnp
from jax import lax
from jax.experimental import pallas as pl
from jax.experimental.pallas import tpu as pltpu
from jax.sharding import PartitionSpec as P

bf16 = jnp.bfloat16
f32 = jnp.float32
VMEM = pltpu.VMEM
PARAMS = pltpu.CompilerParams(vmem_limit_bytes=4 * 2 ** 20)
TASKS = 16


def vmem_spec():
    return pl.BlockSpec(memory_space=VMEM)


def smem_spec():
    return pl.BlockSpec(memory_space=pltpu.SMEM)


def hbm_spec():
    return pl.BlockSpec(memory_space=pltpu.HBM)


def in_vmem(x):
    return pltpu.with_memory_space_constraint(x, VMEM)


def in_hbm(x):
    return pltpu.with_memory_space_constraint(x, pltpu.HBM)


def nn(a, w):
    return lax.dot_general(a, w, (((1,), (0,)), ((), ())), preferred_element_type=f32)


def sigmoid(z):
    return 1.0 / (1.0 + jnp.exp(-z))


def idle_task(t, start, micro):
    return jnp.where(t < start, t, t - micro)


def load_kernel(section, replica, slots, anchors, gain, base, sent, gv, *rest):
    sems = rest[-1]
    micro = base.shape[0]
    copies = [
        pltpu.make_async_copy(gain, gv, sems.at[0]),
    ]
    for m in range(micro):
        copies.append(pltpu.make_async_copy(anchors.at[0, 0, slots[m]], base.at[m], sems.at[1 + m]))
        copies.append(pltpu.make_async_copy(anchors.at[0, 1, slots[m]], sent.at[m], sems.at[1 + micro + m]))
    for c in copies:
        c.start()
    for c in copies:
        c.wait()


def load(section, replica, slots, anchors, gain, state):
    micro = slots.shape[0]
    seq, width = anchors.shape[3:]
    shapes = [
        VMEM((micro, seq, width), bf16),
        VMEM((micro, seq, width), bf16),
        VMEM((1, width), f32),
    ] + [VMEM(shape, dtype) for shape, dtype in state]
    out = pl.pallas_call(
        load_kernel,
        name="load",
        compiler_params=PARAMS,
        out_shape=shapes,
        in_specs=[smem_spec()] * 3 + [hbm_spec()] * 2,
        out_specs=[vmem_spec()] * len(shapes),
        scratch_shapes=[pltpu.SemaphoreType.DMA((1 + 2 * micro,))],
    )(section, replica, slots, *[in_hbm(v) for v in (anchors, gain)])
    return out[:3], out[3:]


def load_weights_kernel(place, w_down, w_up, wd, wu, sems):
    copies = [
        pltpu.make_async_copy(w_down.at[0], wd, sems.at[0]),
        pltpu.make_async_copy(w_up.at[0], wu, sems.at[1]),
    ]
    for c in copies:
        c.start()
    for c in copies:
        c.wait()


def load_weights(gv, w_down, w_up):
    return pl.pallas_call(
        load_weights_kernel,
        name="weights",
        compiler_params=PARAMS,
        out_shape=[VMEM(w_down.shape[1:], bf16), VMEM(w_up.shape[1:], bf16)],
        in_specs=[vmem_spec(), hbm_spec(), hbm_spec()],
        out_specs=[vmem_spec()] * 2,
        scratch_shapes=[pltpu.SemaphoreType.DMA((2,))],
    )(in_vmem(gv), in_hbm(w_down), in_hbm(w_up))


def forward_kernel(t, last, section, delta_in, base, sent, gain, wd, wu,
                   x_old, z_old, r_old, a_old, g_old, dyz_old, wdt_old, wut_old,
                   delta_out, x_all, z_all, r_all, a_all, g_all, dyz, wdt, wut):
    s = section[0]
    m = t - 2 * s
    micro, seq, width = base.shape
    rank = wd.shape[1]
    share = width // dyz.shape[0]
    cols = [(d, slice(d * share, (d + 1) * share)) for d in range(dyz.shape[0])]
    busy = (m >= 0) & (m < micro)
    task = idle_task(t, 2 * s, micro)

    @pl.when(jnp.logical_not(busy) & (task < TASKS))
    def _():
        step = width // TASKS
        part = pl.ds(pl.multiple_of(task * step, step), step)
        wut[part, :] = wu[:, part].T
        wdt[:, part] = wd[part, :].T

    @pl.when(busy)
    def _():
        total = jnp.zeros((seq, 128), f32)
        for d, c in cols:
            x = (base[m, :, c].astype(f32) + delta_in[:, c].astype(f32)).astype(bf16)
            x_all[m, :, c] = x
            h = x.astype(f32)
            sq = h * h
            for k in range(0, share, 128):
                total = total + sq[:, k:k + 128]
        r = lax.rsqrt(jnp.sum(total, -1, keepdims=True) / width + 1e-05)
        r_all[m] = jnp.broadcast_to(r, (seq, 128))
        z = None
        for d, c in cols:
            a = (x_all[m, :, c].astype(f32) * r * gain[:, c]).astype(bf16)
            a_all[m, :, c] = a
            part = nn(a, wd[c, :])
            z = part if z is None else z + part
        z_all[m] = z
        g = (z * sigmoid(z)).astype(bf16)
        g_all[m] = g
        for d, c in cols:
            y = (x_all[m, :, c].astype(f32) + nn(g, wu[:, c])).astype(bf16)
            delta_out[:, c] = (y.astype(f32) - sent[m, :, c].astype(f32)).astype(bf16)

        @pl.when(s == last)
        def _():
            for d, c in cols:
                dyz[d, m, :, :share] = delta_out[:, c]


def forward_step(t, last, section, delta, base, sent, gain, wd, wu, state):
    micro, seq, width = base.shape
    rank = wd.shape[1]
    out = pl.pallas_call(
        lambda *refs: forward_kernel(t, last, *refs),
        name="forward",
        compiler_params=PARAMS,
        out_shape=[jax.ShapeDtypeStruct((seq, width), bf16)] + [VMEM(v.shape, v.dtype) for v in state],
        in_specs=[smem_spec()] + [vmem_spec()] * (6 + len(state)),
        out_specs=[vmem_spec()] * (1 + len(state)),
        input_output_aliases={7 + i: 1 + i for i in range(len(state))},
        cost_estimate=pl.CostEstimate(flops=4 * seq * width * rank, bytes_accessed=2 ** 20, transcendentals=0),
    )(section, delta, *[in_vmem(v) for v in (base, sent, gain, wd, wu, *state)])
    return out[0], out[1:]


def of_section(values, s):
    found = jnp.int32(0)
    for i, v in enumerate(values):
        if v:
            found = jnp.where(s == i, jnp.int32(v), found)
    return found


def backward_kernel(t, last, kinds, section, replica, dy_in, gain, wdt, wut, x_all, z_all, r_all, a_all, g_all,
                    dyz_old, at_old, gt_old, dx_out, dyz, at, gt):
    s, q = section[0], replica[0]
    m = t - 2 * (last - s)
    micro, seq, width = x_all.shape
    rank = wdt.shape[0]
    replicas = dyz.shape[0]
    share = width // replicas
    rows = micro * seq
    cols = [(d, slice(d * share, (d + 1) * share)) for d in range(replicas)]
    busy = (m >= 0) & (m < micro)

    def share_of(d):
        return pl.ds(pl.multiple_of(d * share, share), share)

    def rows_of(d):
        return pl.ds(pl.multiple_of(d * rows, rows), rows)

    if t >= 2 and any(kinds[t - 2]):
        came = of_section(kinds[t - 2], s)
        source = lax.rem(q + replicas - came // 4, replicas)

        @pl.when(came % 4 == 1)
        def _():
            block = jnp.concatenate([dy_in[:, i * share:(i + 1) * share] for i in range(micro)], 0)
            at[:, rows_of(source)] = block.T

        @pl.when(came % 4 == 2)
        def _():
            block = jnp.concatenate([dy_in[:, i * rank:(i + 1) * rank] for i in range(micro)], 0)
            gt[:, rows_of(source)] = block.T

    if any(kinds[t]):
        goes = of_section(kinds[t], s)
        target = lax.rem(q + goes // 4, replicas)

        @pl.when(goes % 4 == 1)
        def _():
            for i in range(micro):
                dx_out[:, i * share:(i + 1) * share] = a_all[i, :, share_of(target)]

        @pl.when(goes % 4 == 2)
        def _():
            for i in range(micro):
                dx_out[:, i * rank:(i + 1) * rank] = g_all[i]

        if any(v == 3 for v in kinds[t]):
            @pl.when(goes == 3)
            def _():
                at[:, rows_of(q)] = jnp.concatenate([a_all[i, :, share_of(q)] for i in range(micro)], 0).T
                gt[:, rows_of(q)] = jnp.concatenate([g_all[i] for i in range(micro)], 0).T

    @pl.when(busy)
    def _():
        dg = None
        for d, c in cols:
            dy = dy_in[:, c]
            if t < micro:
                dy = jnp.where(s == last, dyz[d, m, :, :share], dy)
            dyz[d, m, :, :share] = dy
            part = nn(dy, wut[c, :])
            dg = part if dg is None else dg + part
        z = z_all[m]
        sig = sigmoid(z)
        dz = (dg * sig * (1.0 + z * (1.0 - sig))).astype(bf16)
        for d, c in cols:
            dyz[d, m, :, share:] = dz

        @pl.when(s > 0)
        def _():
            r = r_all[m][:, :1]
            coef = r * r * (jnp.sum(dz.astype(f32) * z, -1, keepdims=True) / width)
            for d, c in cols:
                u = nn(dz, wdt[:, c]) * gain[:, c]
                dx = dyz[d, m, :, :share].astype(f32) + r * u - x_all[m, :, c].astype(f32) * coef
                dx_out[:, c] = dx.astype(bf16)


def backward_step(t, last, kinds, section, replica, dy, fixed, state):
    gain, wdt, wut, x_all = fixed[:4]
    micro, seq, width = x_all.shape
    rank = wdt.shape[0]
    out = pl.pallas_call(
        lambda *refs: backward_kernel(t, last, kinds, *refs),
        name="backward",
        compiler_params=PARAMS,
        out_shape=[jax.ShapeDtypeStruct((seq, width), bf16)] + [VMEM(v.shape, v.dtype) for v in state],
        in_specs=[smem_spec()] * 2 + [vmem_spec()] * 12,
        out_specs=[vmem_spec()] * 4,
        input_output_aliases={11: 1, 12: 2, 13: 3},
        cost_estimate=pl.CostEstimate(flops=4 * seq * width * rank, bytes_accessed=2 ** 20, transcendentals=0),
    )(section, replica, dy, *[in_vmem(v) for v in fixed], *[in_vmem(v) for v in state])
    return out[0], out[1:]


def keep_kernel(owner, anchors, x_all, kept, held, arrive, leave):
    slots = kept.shape[1]
    for j in range(slots):
        @pl.when(owner[j] >= 0)
        def _():
            pltpu.make_async_copy(x_all.at[owner[j]], held.at[j], arrive.at[j]).start()

        @pl.when(owner[j] < 0)
        def _():
            pltpu.make_async_copy(anchors.at[0, 0, j], held.at[j], arrive.at[j]).start()
    out = [pltpu.make_async_copy(held.at[j], kept.at[0, j], leave.at[j]) for j in range(slots)]
    for j in range(slots):
        pltpu.make_async_copy(anchors.at[0, 0, j], held.at[j], arrive.at[j]).wait()
        out[j].start()
    for copy in out:
        copy.wait()


def keep(owner, anchors, x_all):
    slots, seq, width = anchors.shape[2:]
    return pl.pallas_call(
        keep_kernel,
        name="keep",
        compiler_params=pltpu.CompilerParams(vmem_limit_bytes=8 * 2 ** 20),
        out_shape=pltpu.HBM((1, slots, seq, width), bf16),
        in_specs=[smem_spec(), hbm_spec(), hbm_spec()],
        out_specs=hbm_spec(),
        scratch_shapes=[VMEM((slots, seq, width), bf16)] + [pltpu.SemaphoreType.DMA((slots,))] * 2,
    )(owner, in_hbm(anchors), in_hbm(x_all))


def pack_kernel(dyz, out, sem):
    copy = pltpu.make_async_copy(dyz, out, sem)
    copy.start()
    copy.wait()


def pack(dyz):
    return pl.pallas_call(
        pack_kernel,
        name="pack",
        compiler_params=PARAMS,
        out_shape=pltpu.HBM(dyz.shape, bf16),
        in_specs=[vmem_spec()],
        out_specs=hbm_spec(),
        scratch_shapes=[pltpu.SemaphoreType.DMA],
    )(in_vmem(dyz))


def gradients_kernel(at, gt, dyz, down, up):
    share = at.shape[0]
    rank = gt.shape[0]
    block = 512

    def down_rows(i, _):
        part = pl.ds(pl.multiple_of(i * block, block), block)
        down[part, :] = nn(at[part, :], dyz[:, share:]).astype(bf16)
        return 0

    def up_rows(i, _):
        part = pl.ds(pl.multiple_of(i * block, block), block)
        up[part, :] = nn(gt[part, :], dyz[:, :share]).astype(bf16)
        return 0

    lax.fori_loop(0, share // block, down_rows, 0)
    lax.fori_loop(0, rank // block, up_rows, 0)


def gradients(at, gt, dyz):
    share, rows = at.shape
    rank = gt.shape[0]
    return pl.pallas_call(
        gradients_kernel,
        name="gradients",
        compiler_params=pltpu.CompilerParams(vmem_limit_bytes=24 * 2 ** 20),
        out_shape=[jax.ShapeDtypeStruct((share, rank), bf16), jax.ShapeDtypeStruct((rank, share), bf16)],
        in_specs=[vmem_spec()] * 3,
        out_specs=[vmem_spec()] * 2,
    )(in_vmem(at), in_vmem(gt), dyz)


def empty(shapes):
    return pl.pallas_call(
        lambda *o: None, name="empty", compiler_params=PARAMS, out_shape=[VMEM(*v) for v in shapes],
        out_specs=[vmem_spec()] * len(shapes)
    )()


def hops(t, last, steps, micro):
    final = (steps - 1) // 2 - 2
    k = t // 2
    low = 0 if k < 3 else min((k - 1) // 2 * 2 + 1, final - 2)
    high = low + 2 if low == 0 or low + 2 >= final else low + 1
    return low, [s for s in range(max(0, low - micro // 2 + 1), min(last - 1, high) + 1)]


def ride(last, steps, micro, replicas):
    groups = [hops(t, last, steps, micro) for t in range(steps - 2)]
    taken = [{last - s for s in senders} | {last - s - 1 for s in senders} for _, senders in groups]
    sent = []
    for s in range(last + 1):
        free = [(low, t % 2) for t, (low, _) in enumerate(groups) if s not in taken[t]]
        free = list(dict.fromkeys(free))
        late = [v for v in free if v[0] > last - s]
        late = late[:replicas - 1]
        early = [v for v in free if v[0] <= last - s][:replicas - 1 - len(late)]
        sent.append({v: [i + 1, 0] for i, v in enumerate(early + late)})
    pairs, kinds = [], []
    for t in range(steps):
        kind = [0] * (last + 1)
        perm = []
        if t < steps - 2:
            low, senders = groups[t]
            for s in senders:
                perm += [((last - s) * replicas + q, (last - s - 1) * replicas + q) for q in range(replicas)]
            for s in range(last + 1):
                slot = (low, t % 2)
                if slot in sent[s]:
                    distance, count = sent[s][slot]
                    perm += [(s * replicas + q, s * replicas + (q + distance) % replicas) for q in range(replicas)]
                    if count < 2:
                        kind[s] = 4 * distance + count + 1
                        sent[s][slot][1] += 1
        pairs.append(perm)
        kinds.append(kind)
    for s in range(last + 1):
        assert sorted(v[0] for v in sent[s].values()) == list(range(1, replicas))
        assert all(v[1] == 2 for v in sent[s].values())
        free = [t for t in range(steps) if kinds[t][s] == 0 and not 0 <= t - 2 * (last - s) < micro]
        kinds[free[-1]][s] = 3
    return pairs, kinds


def shards(anchors, sample_ids, gain, w_down, w_up):
    section = jnp.full((1,), lax.axis_index("section"), jnp.int32)
    replica = jnp.full((1,), lax.axis_index("dp"), jnp.int32)
    sections = lax.axis_size("section")
    replicas = lax.axis_size("dp")
    slots = sample_ids[0]
    micro = slots.shape[0]
    store, seq, width = anchors.shape[2:]
    rank = w_down.shape[2]
    last = sections - 1
    steps = micro + 2 * last
    rows = micro * seq
    share = width // replicas
    pairs, kinds = ride(last, steps, micro, replicas)
    match = slots[None, :] == jnp.arange(store, dtype=jnp.int32)[:, None]
    owner = jnp.max(jnp.where(match, jnp.arange(micro, dtype=jnp.int32)[None, :], -1), 1).astype(jnp.int32)
    nothing = jnp.zeros((seq, width), bf16)
    slots, owner, nothing = lax.optimization_barrier((slots, owner, nothing))

    (base, sent, gv), state = load(section, replica, slots, anchors, gain, [
        ((micro, seq, width), bf16),
        ((micro, seq, rank), f32),
        ((micro, seq, 128), f32),
        ((micro, seq, width), bf16),
        ((micro, seq, rank), bf16),
        ((replicas, micro, seq, share + rank), bf16),
        ((rank, width), bf16),
        ((width, rank), bf16),
    ])
    wd, wu = load_weights(gv, w_down, w_up)
    arrived = [nothing, nothing]
    for t in range(steps):
        delta, state = forward_step(t, last, section, arrived[t], base, sent, gv, wd, wu, state)
        if t < steps - 2:
            senders = hops(t, last, steps, micro)[1]
            arrived.append(lax.ppermute(delta, "section", [(s, s + 1) for s in senders]))
    x_all, z_all, r_all, a_all, g_all, dyz, wdt, wut = state

    state = [dyz, *empty([((share, replicas * rows), bf16), ((rank, replicas * rows), bf16)])]
    fixed = [gv, wdt, wut, x_all, z_all, r_all, a_all, g_all]
    arrived = [nothing, nothing]
    for t in range(steps):
        dx, state = backward_step(t, last, kinds, section, replica, arrived[t], fixed, state)
        if t < steps - 2:
            arrived.append(lax.ppermute(dx, ("section", "dp"), pairs[t]))
    dyz, at, gt = state
    dyz, x_all = lax.optimization_barrier((pack(dyz), x_all))
    kept = keep(owner, anchors, x_all)
    dyz = lax.all_to_all(dyz, "dp", 0, 0, tiled=True).reshape(replicas * rows, share + rank)
    grad_down, grad_up = gradients(at, gt, dyz)
    return kept, grad_down[None], grad_up[None]


def solution(mesh):
    placed = (
        P("section", None, "dp", None, None),
        P("dp", None),
        P("section", None),
        P("section", None, None),
        P("section", None, None),
    )
    return jax.shard_map(
        shards,
        mesh=mesh,
        in_specs=placed,
        out_specs=(
            P("section", "dp", None, None),
            P("section", "dp", None),
            P("section", None, "dp"),
        ),
        check_vma=False,
    )
```

```python
import jax
import jax.numpy as jnp
from jax import lax
from jax.experimental import pallas as pl
from jax.experimental.pallas import tpu as pltpu
from jax.sharding import PartitionSpec as P

bf16 = jnp.bfloat16
f32 = jnp.float32
VMEM = pltpu.VMEM
PARAMS = pltpu.CompilerParams(vmem_limit_bytes=2 * 2 ** 20)
TASKS = 16


def vmem_spec():
    return pl.BlockSpec(memory_space=VMEM)


def smem_spec():
    return pl.BlockSpec(memory_space=pltpu.SMEM)


def hbm_spec():
    return pl.BlockSpec(memory_space=pltpu.HBM)


def in_vmem(x):
    return pltpu.with_memory_space_constraint(x, VMEM)


def in_hbm(x):
    return pltpu.with_memory_space_constraint(x, pltpu.HBM)


def nn(a, w):
    return lax.dot_general(a, w, (((1,), (0,)), ((), ())), preferred_element_type=f32)


def sigmoid(z):
    return 1.0 / (1.0 + jnp.exp(-z))


def idle_task(t, start, micro):
    return jnp.where(t < start, t, t - micro)


def load_kernel(section, replica, slots, anchors, gain, base, sent, gv, *rest):
    sems = rest[-1]
    micro = base.shape[0]
    copies = [
        pltpu.make_async_copy(gain, gv, sems.at[0]),
    ]
    for m in range(micro):
        copies.append(pltpu.make_async_copy(anchors.at[0, 0, slots[m]], base.at[m], sems.at[1 + m]))
        copies.append(pltpu.make_async_copy(anchors.at[0, 1, slots[m]], sent.at[m], sems.at[1 + micro + m]))
    for c in copies:
        c.start()
    for c in copies:
        c.wait()


def load(section, replica, slots, anchors, gain, state):
    micro = slots.shape[0]
    seq, width = anchors.shape[3:]
    shapes = [
        VMEM((micro, seq, width), bf16),
        VMEM((micro, seq, width), bf16),
        VMEM((1, width), f32),
    ] + [VMEM(shape, dtype) for shape, dtype in state]
    out = pl.pallas_call(
        load_kernel,
        name="load",
        compiler_params=PARAMS,
        out_shape=shapes,
        in_specs=[smem_spec()] * 3 + [hbm_spec()] * 2,
        out_specs=[vmem_spec()] * len(shapes),
        scratch_shapes=[pltpu.SemaphoreType.DMA((1 + 2 * micro,))],
    )(section, replica, slots, *[in_hbm(v) for v in (anchors, gain)])
    return out[:3], out[3:]


def load_weights_kernel(place, w_down, w_up, wd, wu, sems):
    copies = [
        pltpu.make_async_copy(w_down.at[0], wd, sems.at[0]),
        pltpu.make_async_copy(w_up.at[0], wu, sems.at[1]),
    ]
    for c in copies:
        c.start()
    for c in copies:
        c.wait()


def load_weights(gv, w_down, w_up):
    return pl.pallas_call(
        load_weights_kernel,
        name="weights",
        compiler_params=PARAMS,
        out_shape=[VMEM(w_down.shape[1:], bf16), VMEM(w_up.shape[1:], bf16)],
        in_specs=[vmem_spec(), hbm_spec(), hbm_spec()],
        out_specs=[vmem_spec()] * 2,
        scratch_shapes=[pltpu.SemaphoreType.DMA((2,))],
    )(in_vmem(gv), in_hbm(w_down), in_hbm(w_up))


def forward_kernel(t, last, section, delta_in, base, sent, gain, wd, wu,
                   x_old, z_old, r_old, a_old, g_old, dyz_old, wdt_old, wut_old,
                   delta_out, x_all, z_all, r_all, a_all, g_all, dyz, wdt, wut):
    s = section[0]
    m = t - 2 * s
    micro, seq, width = base.shape
    rank = wd.shape[1]
    share = width // dyz.shape[0]
    cols = [(d, slice(d * share, (d + 1) * share)) for d in range(dyz.shape[0])]
    busy = (m >= 0) & (m < micro)
    task = idle_task(t, 2 * s, micro)

    @pl.when(jnp.logical_not(busy) & (task < TASKS))
    def _():
        step = width // TASKS
        part = pl.ds(pl.multiple_of(task * step, step), step)
        wut[part, :] = wu[:, part].T
        wdt[:, part] = wd[part, :].T

    @pl.when(busy)
    def _():
        total = jnp.zeros((seq, 128), f32)
        for d, c in cols:
            x = (base[m, :, c].astype(f32) + delta_in[:, c].astype(f32)).astype(bf16)
            x_all[m, :, c] = x
            h = x.astype(f32)
            sq = h * h
            for k in range(0, share, 128):
                total = total + sq[:, k:k + 128]
        r = lax.rsqrt(jnp.sum(total, -1, keepdims=True) / width + 1e-05)
        r_all[m] = jnp.broadcast_to(r, (seq, 128))
        z = None
        for d, c in cols:
            a = (x_all[m, :, c].astype(f32) * r * gain[:, c]).astype(bf16)
            a_all[m, :, c] = a
            part = nn(a, wd[c, :])
            z = part if z is None else z + part
        z_all[m] = z
        g = (z * sigmoid(z)).astype(bf16)
        g_all[m] = g
        for d, c in cols:
            y = (x_all[m, :, c].astype(f32) + nn(g, wu[:, c])).astype(bf16)
            delta_out[:, c] = (y.astype(f32) - sent[m, :, c].astype(f32)).astype(bf16)

        @pl.when(s == last)
        def _():
            for d, c in cols:
                dyz[d, m, :, :share] = delta_out[:, c]


def forward_step(t, last, section, delta, base, sent, gain, wd, wu, state):
    micro, seq, width = base.shape
    rank = wd.shape[1]
    out = pl.pallas_call(
        lambda *refs: forward_kernel(t, last, *refs),
        name="forward",
        compiler_params=PARAMS,
        out_shape=[jax.ShapeDtypeStruct((seq, width), bf16)] + [VMEM(v.shape, v.dtype) for v in state],
        in_specs=[smem_spec()] + [vmem_spec()] * (6 + len(state)),
        out_specs=[vmem_spec()] * (1 + len(state)),
        input_output_aliases={7 + i: 1 + i for i in range(len(state))},
        cost_estimate=pl.CostEstimate(flops=4 * seq * width * rank, bytes_accessed=2 ** 20, transcendentals=0),
    )(section, delta, *[in_vmem(v) for v in (base, sent, gain, wd, wu, *state)])
    return out[0], out[1:]


def of_section(values, s):
    found = jnp.int32(0)
    for i, v in enumerate(values):
        if v:
            found = jnp.where(s == i, jnp.int32(v), found)
    return found


def backward_kernel(t, last, kinds, section, replica, dy_in, gain, wdt, wut, x_all, z_all, r_all, a_all, g_all,
                    dyz_old, at_old, gt_old, dx_out, dyz, at, gt):
    s, q = section[0], replica[0]
    m = t - 2 * (last - s)
    micro, seq, width = x_all.shape
    rank = wdt.shape[0]
    replicas = dyz.shape[0]
    share = width // replicas
    rows = micro * seq
    cols = [(d, slice(d * share, (d + 1) * share)) for d in range(replicas)]
    busy = (m >= 0) & (m < micro)

    def share_of(d):
        return pl.ds(pl.multiple_of(d * share, share), share)

    def rows_of(d):
        return pl.ds(pl.multiple_of(d * rows, rows), rows)

    if t >= 2 and any(kinds[t - 2]):
        came = of_section(kinds[t - 2], s)
        source = lax.rem(q + replicas - came // 4, replicas)

        @pl.when(came % 4 == 1)
        def _():
            block = jnp.concatenate([dy_in[:, i * share:(i + 1) * share] for i in range(micro)], 0)
            at[:, rows_of(source)] = block.T

        @pl.when(came % 4 == 2)
        def _():
            block = jnp.concatenate([dy_in[:, i * rank:(i + 1) * rank] for i in range(micro)], 0)
            gt[:, rows_of(source)] = block.T

    if any(kinds[t]):
        goes = of_section(kinds[t], s)
        target = lax.rem(q + goes // 4, replicas)

        @pl.when(goes % 4 == 1)
        def _():
            for i in range(micro):
                dx_out[:, i * share:(i + 1) * share] = a_all[i, :, share_of(target)]

        @pl.when(goes % 4 == 2)
        def _():
            for i in range(micro):
                dx_out[:, i * rank:(i + 1) * rank] = g_all[i]

        if any(v == 3 for v in kinds[t]):
            @pl.when(goes == 3)
            def _():
                at[:, rows_of(q)] = jnp.concatenate([a_all[i, :, share_of(q)] for i in range(micro)], 0).T
                gt[:, rows_of(q)] = jnp.concatenate([g_all[i] for i in range(micro)], 0).T

    @pl.when(busy)
    def _():
        dg = None
        for d, c in cols:
            dy = dy_in[:, c]
            if t < micro:
                dy = jnp.where(s == last, dyz[d, m, :, :share], dy)
            dyz[d, m, :, :share] = dy
            part = nn(dy, wut[c, :])
            dg = part if dg is None else dg + part
        z = z_all[m]
        sig = sigmoid(z)
        dz = (dg * sig * (1.0 + z * (1.0 - sig))).astype(bf16)
        for d, c in cols:
            dyz[d, m, :, share:] = dz

        @pl.when(s > 0)
        def _():
            r = r_all[m][:, :1]
            coef = r * r * (jnp.sum(dz.astype(f32) * z, -1, keepdims=True) / width)
            for d, c in cols:
                u = nn(dz, wdt[:, c]) * gain[:, c]
                dx = dyz[d, m, :, :share].astype(f32) + r * u - x_all[m, :, c].astype(f32) * coef
                dx_out[:, c] = dx.astype(bf16)


def backward_step(t, last, kinds, section, replica, dy, fixed, state):
    gain, wdt, wut, x_all = fixed[:4]
    micro, seq, width = x_all.shape
    rank = wdt.shape[0]
    out = pl.pallas_call(
        lambda *refs: backward_kernel(t, last, kinds, *refs),
        name="backward",
        compiler_params=PARAMS,
        out_shape=[jax.ShapeDtypeStruct((seq, width), bf16)] + [VMEM(v.shape, v.dtype) for v in state],
        in_specs=[smem_spec()] * 2 + [vmem_spec()] * 12,
        out_specs=[vmem_spec()] * 4,
        input_output_aliases={11: 1, 12: 2, 13: 3},
        cost_estimate=pl.CostEstimate(flops=4 * seq * width * rank, bytes_accessed=2 ** 20, transcendentals=0),
    )(section, replica, dy, *[in_vmem(v) for v in fixed], *[in_vmem(v) for v in state])
    return out[0], out[1:]


def keep_kernel(owner, anchors, x_all, kept, held, arrive, leave):
    slots = kept.shape[1]
    for j in range(slots):
        @pl.when(owner[j] >= 0)
        def _():
            pltpu.make_async_copy(x_all.at[owner[j]], held.at[j], arrive.at[j]).start()

        @pl.when(owner[j] < 0)
        def _():
            pltpu.make_async_copy(anchors.at[0, 0, j], held.at[j], arrive.at[j]).start()
    out = [pltpu.make_async_copy(held.at[j], kept.at[0, j], leave.at[j]) for j in range(slots)]
    for j in range(slots):
        pltpu.make_async_copy(anchors.at[0, 0, j], held.at[j], arrive.at[j]).wait()
        out[j].start()
    for copy in out:
        copy.wait()


def keep(owner, anchors, x_all):
    slots, seq, width = anchors.shape[2:]
    return pl.pallas_call(
        keep_kernel,
        name="keep",
        compiler_params=pltpu.CompilerParams(vmem_limit_bytes=8 * 2 ** 20),
        out_shape=pltpu.HBM((1, slots, seq, width), bf16),
        in_specs=[smem_spec(), hbm_spec(), hbm_spec()],
        out_specs=hbm_spec(),
        scratch_shapes=[VMEM((slots, seq, width), bf16)] + [pltpu.SemaphoreType.DMA((slots,))] * 2,
    )(owner, in_hbm(anchors), in_hbm(x_all))


def pack_kernel(dyz, out, sem):
    copy = pltpu.make_async_copy(dyz, out, sem)
    copy.start()
    copy.wait()


def pack(dyz):
    return pl.pallas_call(
        pack_kernel,
        name="pack",
        compiler_params=PARAMS,
        out_shape=pltpu.HBM(dyz.shape, bf16),
        in_specs=[vmem_spec()],
        out_specs=hbm_spec(),
        scratch_shapes=[pltpu.SemaphoreType.DMA],
    )(in_vmem(dyz))


def gradients_kernel(at, gt, dyz, down, up):
    share = at.shape[0]
    rank = gt.shape[0]
    block = 512

    def down_rows(i, _):
        part = pl.ds(pl.multiple_of(i * block, block), block)
        down[part, :] = nn(at[part, :], dyz[:, share:]).astype(bf16)
        return 0

    def up_rows(i, _):
        part = pl.ds(pl.multiple_of(i * block, block), block)
        up[part, :] = nn(gt[part, :], dyz[:, :share]).astype(bf16)
        return 0

    lax.fori_loop(0, share // block, down_rows, 0)
    lax.fori_loop(0, rank // block, up_rows, 0)


def gradients(at, gt, dyz):
    share, rows = at.shape
    rank = gt.shape[0]
    return pl.pallas_call(
        gradients_kernel,
        name="gradients",
        compiler_params=pltpu.CompilerParams(vmem_limit_bytes=24 * 2 ** 20),
        out_shape=[jax.ShapeDtypeStruct((share, rank), bf16), jax.ShapeDtypeStruct((rank, share), bf16)],
        in_specs=[vmem_spec()] * 3,
        out_specs=[vmem_spec()] * 2,
    )(in_vmem(at), in_vmem(gt), dyz)


def empty(shapes):
    return pl.pallas_call(
        lambda *o: None, name="empty", compiler_params=PARAMS, out_shape=[VMEM(*v) for v in shapes],
        out_specs=[vmem_spec()] * len(shapes)
    )()


def hops(t, last, steps, micro):
    final = (steps - 1) // 2 - 2
    k = t // 2
    low = 0 if k < 3 else min((k - 1) // 2 * 2 + 1, final - 2)
    high = low + 2 if low == 0 or low + 2 >= final else low + 1
    return low, [s for s in range(max(0, low - micro // 2 + 1), min(last - 1, high) + 1)]


def ride(last, steps, micro, replicas):
    groups = [hops(t, last, steps, micro) for t in range(steps - 2)]
    taken = [{last - s for s in senders} | {last - s - 1 for s in senders} for _, senders in groups]
    sent = []
    for s in range(last + 1):
        free = [(low, t % 2) for t, (low, _) in enumerate(groups) if s not in taken[t]]
        free = list(dict.fromkeys(free))
        final = {v[0]: max(t for t, (low, _) in enumerate(groups) if low == v[0]) for v in free}
        early = [v for v in free if final[v[0]] <= 2 * (last - s) - 3]
        late = [v for v in free if v[0] > last - s]
        early = early[:replicas - 1]
        late = late[:replicas - 1 - len(early)]
        sent.append({v: [i + 1, 0] for i, v in enumerate(early + late)})
    pairs, kinds = [], []
    for t in range(steps):
        kind = [0] * (last + 1)
        perm = []
        if t < steps - 2:
            low, senders = groups[t]
            for s in senders:
                perm += [((last - s) * replicas + q, (last - s - 1) * replicas + q) for q in range(replicas)]
            for s in range(last + 1):
                slot = (low, t % 2)
                if slot in sent[s]:
                    distance, count = sent[s][slot]
                    perm += [(s * replicas + q, s * replicas + (q + distance) % replicas) for q in range(replicas)]
                    if count < 2:
                        kind[s] = 4 * distance + count + 1
                        sent[s][slot][1] += 1
        pairs.append(perm)
        kinds.append(kind)
    for s in range(last + 1):
        assert sorted(v[0] for v in sent[s].values()) == list(range(1, replicas))
        assert all(v[1] == 2 for v in sent[s].values())
        free = [t for t in range(steps) if kinds[t][s] == 0 and not 0 <= t - 2 * (last - s) < micro]
        kinds[free[-1]][s] = 3
    return pairs, kinds


def shards(anchors, sample_ids, gain, w_down, w_up):
    section = jnp.full((1,), lax.axis_index("section"), jnp.int32)
    replica = jnp.full((1,), lax.axis_index("dp"), jnp.int32)
    sections = lax.axis_size("section")
    replicas = lax.axis_size("dp")
    slots = sample_ids[0]
    micro = slots.shape[0]
    store, seq, width = anchors.shape[2:]
    rank = w_down.shape[2]
    last = sections - 1
    steps = micro + 2 * last
    rows = micro * seq
    share = width // replicas
    pairs, kinds = ride(last, steps, micro, replicas)
    match = slots[None, :] == jnp.arange(store, dtype=jnp.int32)[:, None]
    owner = jnp.max(jnp.where(match, jnp.arange(micro, dtype=jnp.int32)[None, :], -1), 1).astype(jnp.int32)
    nothing = jnp.zeros((seq, width), bf16)
    slots, owner, nothing = lax.optimization_barrier((slots, owner, nothing))

    (base, sent, gv), state = load(section, replica, slots, anchors, gain, [
        ((micro, seq, width), bf16),
        ((micro, seq, rank), f32),
        ((micro, seq, 128), f32),
        ((micro, seq, width), bf16),
        ((micro, seq, rank), bf16),
        ((replicas, micro, seq, share + rank), bf16),
        ((rank, width), bf16),
        ((width, rank), bf16),
        ((share, replicas * rows), bf16),
        ((rank, replicas * rows), bf16),
    ])
    state, (at, gt) = state[:8], state[8:]
    wd, wu = load_weights(gv, w_down, w_up)
    arrived = [nothing, nothing]
    for t in range(steps):
        delta, state = forward_step(t, last, section, arrived[t], base, sent, gv, wd, wu, state)
        if t < steps - 2:
            senders = hops(t, last, steps, micro)[1]
            arrived.append(lax.ppermute(delta, "section", [(s, s + 1) for s in senders]))
    x_all, z_all, r_all, a_all, g_all, dyz, wdt, wut = state

    state = [dyz, at, gt]
    fixed = [gv, wdt, wut, x_all, z_all, r_all, a_all, g_all]
    arrived = [nothing, nothing]
    for t in range(steps):
        dx, state = backward_step(t, last, kinds, section, replica, arrived[t], fixed, state)
        if t < steps - 2:
            arrived.append(lax.ppermute(dx, ("section", "dp"), pairs[t]))
    dyz, at, gt = state
    dyz, x_all = lax.optimization_barrier((pack(dyz), x_all))
    kept = keep(owner, anchors, x_all)
    dyz = lax.all_to_all(dyz, "dp", 0, 0, tiled=True).reshape(replicas * rows, share + rank)
    grad_down, grad_up = gradients(at, gt, dyz)
    return kept, grad_down[None], grad_up[None]


def solution(mesh):
    placed = (
        P("section", None, "dp", None, None),
        P("dp", None),
        P("section", None),
        P("section", None, None),
        P("section", None, None),
    )
    return jax.shard_map(
        shards,
        mesh=mesh,
        in_specs=placed,
        out_specs=(
            P("section", "dp", None, None),
            P("section", "dp", None),
            P("section", None, "dp"),
        ),
        check_vma=False,
    )
```

```python
import jax
import jax.numpy as jnp
from jax import lax
from jax.experimental import pallas as pl
from jax.experimental.pallas import tpu as pltpu
from jax.sharding import PartitionSpec as P

bf16 = jnp.bfloat16
f32 = jnp.float32
VMEM = pltpu.VMEM
PARAMS = pltpu.CompilerParams(vmem_limit_bytes=2 * 2 ** 20)
TASKS = 16


def vmem_spec():
    return pl.BlockSpec(memory_space=VMEM)


def smem_spec():
    return pl.BlockSpec(memory_space=pltpu.SMEM)


def hbm_spec():
    return pl.BlockSpec(memory_space=pltpu.HBM)


def in_vmem(x):
    return pltpu.with_memory_space_constraint(x, VMEM)


def in_hbm(x):
    return pltpu.with_memory_space_constraint(x, pltpu.HBM)


def nn(a, w):
    return lax.dot_general(a, w, (((1,), (0,)), ((), ())), preferred_element_type=f32)


def sigmoid(z):
    return 1.0 / (1.0 + jnp.exp(-z))


def idle_task(t, start, micro):
    return jnp.where(t < start, t, t - micro)


def load_kernel(section, replica, slots, anchors, gain, gv, x_all, dyz, *rest):
    sems = rest[-1]
    micro = x_all.shape[0]
    replicas = dyz.shape[0]
    share = x_all.shape[2] // replicas
    copies = [pltpu.make_async_copy(gain, gv, sems.at[0])]
    for m in range(micro):
        copies.append(pltpu.make_async_copy(anchors.at[0, 0, slots[m]], x_all.at[m], sems.at[1 + m]))
        for d in range(replicas):
            copies.append(pltpu.make_async_copy(
                anchors.at[0, 1, slots[m], :, pl.ds(d * share, share)],
                dyz.at[d, m, :, pl.ds(0, share)],
                sems.at[1 + micro + m * replicas + d]))
    for c in copies:
        c.start()
    for c in copies:
        c.wait()


def load(section, replica, slots, anchors, gain, x_all, dyz, rooms):
    micro = slots.shape[0]
    width = anchors.shape[4]
    shapes = [VMEM((1, width), f32)] + [VMEM(shape, dtype) for shape, dtype in (x_all, dyz, *rooms)]
    return pl.pallas_call(
        load_kernel,
        name="load",
        compiler_params=PARAMS,
        out_shape=shapes,
        in_specs=[smem_spec()] * 3 + [hbm_spec()] * 2,
        out_specs=[vmem_spec()] * len(shapes),
        scratch_shapes=[pltpu.SemaphoreType.DMA((1 + micro + micro * dyz[0][0],))],
    )(section, replica, slots, *[in_hbm(v) for v in (anchors, gain)])


def of_section(values, s):
    found = jnp.int32(0)
    for i, v in enumerate(values):
        if v:
            found = jnp.where(s == i, jnp.int32(v), found)
    return found


def exchange(came, goes, s, q, arrived, out, a_all, g_all, at, gt):
    micro = a_all.shape[0]
    share, total = at.shape
    rank = gt.shape[0]
    rows = micro * a_all.shape[1]
    replicas = total // rows

    def share_of(d):
        return pl.ds(pl.multiple_of(d * share, share), share)

    def rows_of(d):
        return pl.ds(pl.multiple_of(d * rows, rows), rows)

    if any(came):
        code = of_section(came, s)
        source = lax.rem(q + replicas - code // 4, replicas)

        @pl.when(code % 4 == 1)
        def _():
            block = jnp.concatenate([arrived[:, i * share:(i + 1) * share] for i in range(micro)], 0)
            at[:, rows_of(source)] = block.T

        @pl.when(code % 4 == 2)
        def _():
            block = jnp.concatenate([arrived[:, i * rank:(i + 1) * rank] for i in range(micro)], 0)
            gt[:, rows_of(source)] = block.T

    if any(goes):
        send = of_section(goes, s)
        target = lax.rem(q + send // 4, replicas)

        @pl.when(send % 4 == 1)
        def _():
            for i in range(micro):
                out[:, i * share:(i + 1) * share] = a_all[i, :, share_of(target)]

        @pl.when(send % 4 == 2)
        def _():
            for i in range(micro):
                out[:, i * rank:(i + 1) * rank] = g_all[i]

        if any(v == 3 for v in goes):
            @pl.when(send == 3)
            def _():
                at[:, rows_of(q)] = jnp.concatenate([a_all[i, :, share_of(q)] for i in range(micro)], 0).T
                gt[:, rows_of(q)] = jnp.concatenate([g_all[i] for i in range(micro)], 0).T


def load_weights_kernel(place, w_down, w_up, wd, wu, sems):
    copies = [
        pltpu.make_async_copy(w_down.at[0], wd, sems.at[0]),
        pltpu.make_async_copy(w_up.at[0], wu, sems.at[1]),
    ]
    for c in copies:
        c.start()
    for c in copies:
        c.wait()


def load_weights(gv, w_down, w_up):
    return pl.pallas_call(
        load_weights_kernel,
        name="weights",
        compiler_params=PARAMS,
        out_shape=[VMEM(w_down.shape[1:], bf16), VMEM(w_up.shape[1:], bf16)],
        in_specs=[vmem_spec(), hbm_spec(), hbm_spec()],
        out_specs=[vmem_spec()] * 2,
        scratch_shapes=[pltpu.SemaphoreType.DMA((2,))],
    )(in_vmem(gv), in_hbm(w_down), in_hbm(w_up))


def forward_kernel(t, last, came, goes, section, replica, delta_in, gain, wd, wu,
                   x_old, z_old, r_old, a_old, g_old, dyz_old, wdt_old, wut_old, at_old, gt_old,
                   delta_out, x_all, z_all, r_all, a_all, g_all, dyz, wdt, wut, at, gt):
    s, q = section[0], replica[0]
    m = t - 2 * s
    micro, seq, width = x_all.shape
    rank = wd.shape[1]
    share = width // dyz.shape[0]
    cols = [(d, slice(d * share, (d + 1) * share)) for d in range(dyz.shape[0])]
    busy = (m >= 0) & (m < micro)
    task = idle_task(t, 2 * s, micro)
    exchange(came, goes, s, q, delta_in, delta_out, a_all, g_all, at, gt)

    @pl.when(jnp.logical_not(busy) & (task < TASKS))
    def _():
        step = width // TASKS
        part = pl.ds(pl.multiple_of(task * step, step), step)
        wut[part, :] = wu[:, part].T
        wdt[:, part] = wd[part, :].T

    @pl.when(busy)
    def _():
        total = jnp.zeros((seq, 128), f32)
        for d, c in cols:
            x = (x_all[m, :, c].astype(f32) + delta_in[:, c].astype(f32)).astype(bf16)
            x_all[m, :, c] = x
            h = x.astype(f32)
            sq = h * h
            for k in range(0, share, 128):
                total = total + sq[:, k:k + 128]
        r = lax.rsqrt(jnp.sum(total, -1, keepdims=True) / width + 1e-05)
        r_all[m] = jnp.broadcast_to(r, (seq, 128))
        z = None
        for d, c in cols:
            a = (x_all[m, :, c].astype(f32) * r * gain[:, c]).astype(bf16)
            a_all[m, :, c] = a
            part = nn(a, wd[c, :])
            z = part if z is None else z + part
        z_all[m] = z
        g = (z * sigmoid(z)).astype(bf16)
        g_all[m] = g
        for d, c in cols:
            y = (x_all[m, :, c].astype(f32) + nn(g, wu[:, c])).astype(bf16)
            delta_out[:, c] = (y.astype(f32) - dyz[d, m, :, :share].astype(f32)).astype(bf16)

        @pl.when(s == last)
        def _():
            for d, c in cols:
                dyz[d, m, :, :share] = delta_out[:, c]


def forward_step(t, last, came, goes, section, replica, delta, gain, wd, wu, state):
    micro, seq, width = state[0].shape
    rank = wd.shape[1]
    out = pl.pallas_call(
        lambda *refs: forward_kernel(t, last, came, goes, *refs),
        name="forward",
        compiler_params=PARAMS,
        out_shape=[jax.ShapeDtypeStruct((seq, width), bf16)] + [VMEM(v.shape, v.dtype) for v in state],
        in_specs=[smem_spec()] * 2 + [vmem_spec()] * (4 + len(state)),
        out_specs=[vmem_spec()] * (1 + len(state)),
        input_output_aliases={6 + i: 1 + i for i in range(len(state))},
        cost_estimate=pl.CostEstimate(flops=4 * seq * width * rank, bytes_accessed=2 ** 20, transcendentals=0),
    )(section, replica, delta, *[in_vmem(v) for v in (gain, wd, wu, *state)])
    return out[0], out[1:]


def backward_kernel(t, last, came, goes, section, replica, dy_in, gain, wdt, wut, x_all, z_all, r_all, a_all, g_all,
                    dyz_old, at_old, gt_old, dx_out, dyz, at, gt):
    s, q = section[0], replica[0]
    m = t - 2 * (last - s)
    micro, seq, width = x_all.shape
    replicas = dyz.shape[0]
    share = width // replicas
    cols = [(d, slice(d * share, (d + 1) * share)) for d in range(replicas)]
    busy = (m >= 0) & (m < micro)
    exchange(came, goes, s, q, dy_in, dx_out, a_all, g_all, at, gt)

    @pl.when(busy)
    def _():
        dg = None
        for d, c in cols:
            dy = dy_in[:, c]
            if t < micro:
                dy = jnp.where(s == last, dyz[d, m, :, :share], dy)
            dyz[d, m, :, :share] = dy
            part = nn(dy, wut[c, :])
            dg = part if dg is None else dg + part
        z = z_all[m]
        sig = sigmoid(z)
        dz = (dg * sig * (1.0 + z * (1.0 - sig))).astype(bf16)
        for d, c in cols:
            dyz[d, m, :, share:] = dz

        @pl.when(s > 0)
        def _():
            r = r_all[m][:, :1]
            coef = r * r * (jnp.sum(dz.astype(f32) * z, -1, keepdims=True) / width)
            for d, c in cols:
                u = nn(dz, wdt[:, c]) * gain[:, c]
                dx = dyz[d, m, :, :share].astype(f32) + r * u - x_all[m, :, c].astype(f32) * coef
                dx_out[:, c] = dx.astype(bf16)


def backward_step(t, last, came, goes, section, replica, dy, fixed, state):
    gain, wdt, wut, x_all = fixed[:4]
    micro, seq, width = x_all.shape
    rank = wdt.shape[0]
    out = pl.pallas_call(
        lambda *refs: backward_kernel(t, last, came, goes, *refs),
        name="backward",
        compiler_params=PARAMS,
        out_shape=[jax.ShapeDtypeStruct((seq, width), bf16)] + [VMEM(v.shape, v.dtype) for v in state],
        in_specs=[smem_spec()] * 2 + [vmem_spec()] * 12,
        out_specs=[vmem_spec()] * 4,
        input_output_aliases={11: 1, 12: 2, 13: 3},
        cost_estimate=pl.CostEstimate(flops=4 * seq * width * rank, bytes_accessed=2 ** 20, transcendentals=0),
    )(section, replica, dy, *[in_vmem(v) for v in fixed], *[in_vmem(v) for v in state])
    return out[0], out[1:]


def keep_kernel(owner, anchors, x_all, kept, held, arrive, leave):
    slots = kept.shape[1]
    for j in range(slots):
        @pl.when(owner[j] >= 0)
        def _():
            pltpu.make_async_copy(x_all.at[owner[j]], held.at[j], arrive.at[j]).start()

        @pl.when(owner[j] < 0)
        def _():
            pltpu.make_async_copy(anchors.at[0, 0, j], held.at[j], arrive.at[j]).start()
    out = [pltpu.make_async_copy(held.at[j], kept.at[0, j], leave.at[j]) for j in range(slots)]
    for j in range(slots):
        pltpu.make_async_copy(anchors.at[0, 0, j], held.at[j], arrive.at[j]).wait()
        out[j].start()
    for copy in out:
        copy.wait()


def keep(owner, anchors, x_all):
    slots, seq, width = anchors.shape[2:]
    return pl.pallas_call(
        keep_kernel,
        name="keep",
        compiler_params=pltpu.CompilerParams(vmem_limit_bytes=8 * 2 ** 20),
        out_shape=pltpu.HBM((1, slots, seq, width), bf16),
        in_specs=[smem_spec(), hbm_spec(), hbm_spec()],
        out_specs=hbm_spec(),
        scratch_shapes=[VMEM((slots, seq, width), bf16)] + [pltpu.SemaphoreType.DMA((slots,))] * 2,
    )(owner, in_hbm(anchors), in_hbm(x_all))


def pack_kernel(dyz, out, sem):
    copy = pltpu.make_async_copy(dyz, out, sem)
    copy.start()
    copy.wait()


def pack(dyz):
    return pl.pallas_call(
        pack_kernel,
        name="pack",
        compiler_params=PARAMS,
        out_shape=pltpu.HBM(dyz.shape, bf16),
        in_specs=[vmem_spec()],
        out_specs=hbm_spec(),
        scratch_shapes=[pltpu.SemaphoreType.DMA],
    )(in_vmem(dyz))


def gradients_kernel(at, gt, dyz, down, up):
    share = at.shape[0]
    rank = gt.shape[0]
    block = 512

    def down_rows(i, _):
        part = pl.ds(pl.multiple_of(i * block, block), block)
        down[part, :] = nn(at[part, :], dyz[:, share:]).astype(bf16)
        return 0

    def up_rows(i, _):
        part = pl.ds(pl.multiple_of(i * block, block), block)
        up[part, :] = nn(gt[part, :], dyz[:, :share]).astype(bf16)
        return 0

    lax.fori_loop(0, share // block, down_rows, 0)
    lax.fori_loop(0, rank // block, up_rows, 0)


def gradients(at, gt, dyz):
    share, rows = at.shape
    rank = gt.shape[0]
    return pl.pallas_call(
        gradients_kernel,
        name="gradients",
        compiler_params=pltpu.CompilerParams(vmem_limit_bytes=24 * 2 ** 20),
        out_shape=[jax.ShapeDtypeStruct((share, rank), bf16), jax.ShapeDtypeStruct((rank, share), bf16)],
        in_specs=[vmem_spec()] * 3,
        out_specs=[vmem_spec()] * 2,
    )(in_vmem(at), in_vmem(gt), dyz)


def hops(t, last, steps, micro):
    final = (steps - 1) // 2 - 2
    k = t // 2
    low = 0 if k < 3 else min((k - 1) // 2 * 2 + 1, final - 2)
    high = low + 2 if low == 0 or low + 2 >= final else low + 1
    return low, [s for s in range(max(0, low - micro // 2 + 1), min(last - 1, high) + 1)]


def ride(last, steps, micro, replicas):
    groups = [hops(t, last, steps, micro) for t in range(steps - 2)]
    lows = list(dict.fromkeys(low for low, _ in groups))
    first = {low: min(t for t, g in enumerate(groups) if g[0] == low) for low in lows}
    final = {low: max(t for t, g in enumerate(groups) if g[0] == low) for low in lows}
    routes = []
    for back in (False, True):
        def at(s, back=back):
            return last - s if back else s
        routes.append([[(at(s), at(s + 1)) for s in senders] for _, senders in groups])

    def free(back, s):
        return [(back, low, parity) for low in lows for parity in (0, 1)
                if all(s not in pair for pair in routes[back][first[low]])]

    chosen = []
    for s in range(last + 1):
        done = [v for v in free(0, s) if first[v[1]] >= 2 * s + micro]
        late = [v for v in free(1, s) if first[v[1]] >= 2 * (last - s) + micro]
        order = [v for v in done if v[1] != lows[-1]] + [v for v in late if v[1] != lows[-1]]
        order += [v for v in done if v[1] == lows[-1]] + [v for v in late if v[1] == lows[-1]]
        chosen.append({v: [i + 1, 0] for i, v in enumerate(order[:replicas - 1])})
    plans = []
    for back in (0, 1):
        pairs, kinds = [], []
        for t in range(steps):
            kind = [0] * (last + 1)
            perm = []
            if t < steps - 2:
                for i, j in routes[back][t]:
                    perm += [(i * replicas + q, j * replicas + q) for q in range(replicas)]
                for s in range(last + 1):
                    slot = chosen[s].get((back, groups[t][0], t % 2))
                    if slot:
                        perm += [(s * replicas + q, s * replicas + (q + slot[0]) % replicas) for q in range(replicas)]
                        if slot[1] < 2:
                            slot[1] += 1
                            kind[s] = 4 * slot[0] + slot[1]
            pairs.append(perm)
            kinds.append(kind)
        plans.append((pairs, kinds))
    for s in range(last + 1):
        assert sorted(v[0] for v in chosen[s].values()) == list(range(1, replicas))
        assert all(v[1] == 2 for v in chosen[s].values())
        kinds = plans[1][1]
        idle = [t for t in range(steps) if kinds[t][s] == 0 and not 0 <= t - 2 * (last - s) < micro]
        kinds[idle[-1]][s] = 3
    return plans


def shards(anchors, sample_ids, gain, w_down, w_up):
    section = jnp.full((1,), lax.axis_index("section"), jnp.int32)
    replica = jnp.full((1,), lax.axis_index("dp"), jnp.int32)
    sections = lax.axis_size("section")
    replicas = lax.axis_size("dp")
    slots = sample_ids[0]
    micro = slots.shape[0]
    store, seq, width = anchors.shape[2:]
    rank = w_down.shape[2]
    last = sections - 1
    steps = micro + 2 * last
    rows = micro * seq
    share = width // replicas
    (forth, forth_kinds), (back, back_kinds) = ride(last, steps, micro, replicas)
    none = [0] * sections
    match = slots[None, :] == jnp.arange(store, dtype=jnp.int32)[:, None]
    owner = jnp.max(jnp.where(match, jnp.arange(micro, dtype=jnp.int32)[None, :], -1), 1).astype(jnp.int32)
    nothing = jnp.zeros((seq, width), bf16)
    slots, owner, nothing = lax.optimization_barrier((slots, owner, nothing))

    gv, x_all, dyz, *rooms = load(
        section, replica, slots, anchors, gain,
        ((micro, seq, width), bf16),
        ((replicas, micro, seq, share + rank), bf16),
        [
            ((micro, seq, rank), f32),
            ((micro, seq, 128), f32),
            ((micro, seq, width), bf16),
            ((micro, seq, rank), bf16),
            ((rank, width), bf16),
            ((width, rank), bf16),
            ((share, replicas * rows), bf16),
            ((rank, replicas * rows), bf16),
        ])
    state = [x_all, *rooms[:4], dyz, *rooms[4:]]
    wd, wu = load_weights(gv, w_down, w_up)
    arrived = [nothing, nothing]
    for t in range(steps):
        came = forth_kinds[t - 2] if t >= 2 else none
        delta, state = forward_step(
            t, last, came, forth_kinds[t], section, replica, arrived[t], gv, wd, wu, state)
        if t < steps - 2:
            arrived.append(lax.ppermute(delta, ("section", "dp"), forth[t]))
    x_all, z_all, r_all, a_all, g_all, dyz, wdt, wut, at, gt = state

    state = [dyz, at, gt]
    fixed = [gv, wdt, wut, x_all, z_all, r_all, a_all, g_all]
    arrived = [nothing, nothing]
    for t in range(steps):
        came = back_kinds[t - 2] if t >= 2 else none
        dx, state = backward_step(t, last, came, back_kinds[t], section, replica, arrived[t], fixed, state)
        if t < steps - 2:
            arrived.append(lax.ppermute(dx, ("section", "dp"), back[t]))
    dyz, at, gt = state
    dyz, x_all = lax.optimization_barrier((pack(dyz), x_all))
    kept = keep(owner, anchors, x_all)
    dyz = lax.all_to_all(dyz, "dp", 0, 0, tiled=True).reshape(replicas * rows, share + rank)
    grad_down, grad_up = gradients(at, gt, dyz)
    return kept, grad_down[None], grad_up[None]


def solution(mesh):
    placed = (
        P("section", None, "dp", None, None),
        P("dp", None),
        P("section", None),
        P("section", None, None),
        P("section", None, None),
    )
    return jax.shard_map(
        shards,
        mesh=mesh,
        in_specs=placed,
        out_specs=(
            P("section", "dp", None, None),
            P("section", "dp", None),
            P("section", None, "dp"),
        ),
        check_vma=False,
    )
```

```python
import jax
import jax.numpy as jnp
from jax import lax
from jax.experimental import pallas as pl
from jax.experimental.pallas import tpu as pltpu
from jax.sharding import PartitionSpec as P

bf16 = jnp.bfloat16
f32 = jnp.float32
VMEM = pltpu.VMEM
PARAMS = pltpu.CompilerParams(vmem_limit_bytes=2 * 2 ** 20)
TASKS = 16


def vmem_spec():
    return pl.BlockSpec(memory_space=VMEM)


def smem_spec():
    return pl.BlockSpec(memory_space=pltpu.SMEM)


def hbm_spec():
    return pl.BlockSpec(memory_space=pltpu.HBM)


def in_vmem(x):
    return pltpu.with_memory_space_constraint(x, VMEM)


def in_hbm(x):
    return pltpu.with_memory_space_constraint(x, pltpu.HBM)


def nn(a, w):
    return lax.dot_general(a, w, (((1,), (0,)), ((), ())), preferred_element_type=f32)


def sigmoid(z):
    return 1.0 / (1.0 + jnp.exp(-z))


def idle_task(t, start, micro):
    return jnp.where(t < start, t, t - micro)


def load_kernel(section, replica, slots, anchors, gain, gv, x_all, dyz, *rest):
    sems = rest[-1]
    micro = x_all.shape[0]
    replicas = dyz.shape[0]
    share = x_all.shape[2] // replicas
    copies = [pltpu.make_async_copy(gain, gv, sems.at[0])]
    for m in range(micro):
        copies.append(pltpu.make_async_copy(anchors.at[0, 0, slots[m]], x_all.at[m], sems.at[1 + m]))
        for d in range(replicas):
            copies.append(pltpu.make_async_copy(
                anchors.at[0, 1, slots[m], :, pl.ds(d * share, share)],
                dyz.at[d, m, :, pl.ds(0, share)],
                sems.at[1 + micro + m * replicas + d]))
    for c in copies:
        c.start()
    for c in copies:
        c.wait()


def load(section, replica, slots, anchors, gain, x_all, dyz, rooms):
    micro = slots.shape[0]
    width = anchors.shape[4]
    shapes = [VMEM((1, width), f32)] + [VMEM(shape, dtype) for shape, dtype in (x_all, dyz, *rooms)]
    return pl.pallas_call(
        load_kernel,
        name="load",
        compiler_params=PARAMS,
        out_shape=shapes,
        in_specs=[smem_spec()] * 3 + [hbm_spec()] * 2,
        out_specs=[vmem_spec()] * len(shapes),
        scratch_shapes=[pltpu.SemaphoreType.DMA((1 + micro + micro * dyz[0][0],))],
    )(section, replica, slots, *[in_hbm(v) for v in (anchors, gain)])


def of_section(values, s):
    found = jnp.int32(0)
    for i, v in enumerate(values):
        if v:
            found = jnp.where(s == i, jnp.int32(v), found)
    return found


def exchange(came, goes, s, q, arrived, out, a_all, g_all, at, gt):
    micro = a_all.shape[0]
    share, total = at.shape
    rank = gt.shape[0]
    rows = micro * a_all.shape[1]
    replicas = total // rows

    def share_of(d):
        return pl.ds(pl.multiple_of(d * share, share), share)

    def rows_of(d):
        return pl.ds(pl.multiple_of(d * rows, rows), rows)

    if any(came):
        code = of_section(came, s)
        source = lax.rem(q + replicas - code // 4, replicas)

        @pl.when(code % 4 == 1)
        def _():
            block = jnp.concatenate([arrived[:, i * share:(i + 1) * share] for i in range(micro)], 0)
            at[:, rows_of(source)] = block.T

        @pl.when(code % 4 == 2)
        def _():
            block = jnp.concatenate([arrived[:, i * rank:(i + 1) * rank] for i in range(micro)], 0)
            gt[:, rows_of(source)] = block.T

    if any(goes):
        send = of_section(goes, s)
        target = lax.rem(q + send // 4, replicas)

        @pl.when(send % 4 == 1)
        def _():
            for i in range(micro):
                out[:, i * share:(i + 1) * share] = a_all[i, :, share_of(target)]

        @pl.when(send % 4 == 2)
        def _():
            for i in range(micro):
                out[:, i * rank:(i + 1) * rank] = g_all[i]

        if any(v == 3 for v in goes):
            @pl.when(send == 3)
            def _():
                at[:, rows_of(q)] = jnp.concatenate([a_all[i, :, share_of(q)] for i in range(micro)], 0).T
                gt[:, rows_of(q)] = jnp.concatenate([g_all[i] for i in range(micro)], 0).T


def load_weights_kernel(place, w_down, w_up, wd, wu, sems):
    copies = [
        pltpu.make_async_copy(w_down.at[0], wd, sems.at[0]),
        pltpu.make_async_copy(w_up.at[0], wu, sems.at[1]),
    ]
    for c in copies:
        c.start()
    for c in copies:
        c.wait()


def load_weights(gv, w_down, w_up):
    return pl.pallas_call(
        load_weights_kernel,
        name="weights",
        compiler_params=PARAMS,
        out_shape=[VMEM(w_down.shape[1:], bf16), VMEM(w_up.shape[1:], bf16)],
        in_specs=[vmem_spec(), hbm_spec(), hbm_spec()],
        out_specs=[vmem_spec()] * 2,
        scratch_shapes=[pltpu.SemaphoreType.DMA((2,))],
    )(in_vmem(gv), in_hbm(w_down), in_hbm(w_up))


def forward_kernel(t, last, came, goes, section, replica, delta_in, gain, wd, wu,
                   x_old, z_old, r_old, a_old, g_old, dyz_old, wdt_old, wut_old, at_old, gt_old,
                   delta_out, x_all, z_all, r_all, a_all, g_all, dyz, wdt, wut, at, gt):
    s, q = section[0], replica[0]
    m = t - 2 * s
    micro, seq, width = x_all.shape
    rank = wd.shape[1]
    share = width // dyz.shape[0]
    cols = [(d, slice(d * share, (d + 1) * share)) for d in range(dyz.shape[0])]
    busy = (m >= 0) & (m < micro)
    task = idle_task(t, 2 * s, micro)
    exchange(came, goes, s, q, delta_in, delta_out, a_all, g_all, at, gt)

    @pl.when(jnp.logical_not(busy) & (task < TASKS))
    def _():
        step = width // TASKS
        part = pl.ds(pl.multiple_of(task * step, step), step)
        wut[part, :] = wu[:, part].T
        wdt[:, part] = wd[part, :].T

    @pl.when(busy)
    def _():
        total = jnp.zeros((seq, 128), f32)
        for d, c in cols:
            x = (x_all[m, :, c].astype(f32) + delta_in[:, c].astype(f32)).astype(bf16)
            x_all[m, :, c] = x
            h = x.astype(f32)
            sq = h * h
            for k in range(0, share, 128):
                total = total + sq[:, k:k + 128]
        r = lax.rsqrt(jnp.sum(total, -1, keepdims=True) / width + 1e-05)
        r_all[m] = jnp.broadcast_to(r, (seq, 128))
        z = None
        for d, c in cols:
            a = (x_all[m, :, c].astype(f32) * r * gain[:, c]).astype(bf16)
            a_all[m, :, c] = a
            part = nn(a, wd[c, :])
            z = part if z is None else z + part
        z_all[m] = z
        g = (z * sigmoid(z)).astype(bf16)
        g_all[m] = g
        for d, c in cols:
            y = (x_all[m, :, c].astype(f32) + nn(g, wu[:, c])).astype(bf16)
            delta_out[:, c] = (y.astype(f32) - dyz[d, m, :, :share].astype(f32)).astype(bf16)

        @pl.when(s == last)
        def _():
            for d, c in cols:
                dyz[d, m, :, :share] = delta_out[:, c]


def forward_step(t, last, came, goes, section, replica, delta, gain, wd, wu, state):
    micro, seq, width = state[0].shape
    rank = wd.shape[1]
    out = pl.pallas_call(
        lambda *refs: forward_kernel(t, last, came, goes, *refs),
        name="forward",
        compiler_params=PARAMS,
        out_shape=[jax.ShapeDtypeStruct((seq, width), bf16)] + [VMEM(v.shape, v.dtype) for v in state],
        in_specs=[smem_spec()] * 2 + [vmem_spec()] * (4 + len(state)),
        out_specs=[vmem_spec()] * (1 + len(state)),
        input_output_aliases={6 + i: 1 + i for i in range(len(state))},
        cost_estimate=pl.CostEstimate(flops=4 * seq * width * rank, bytes_accessed=2 ** 20, transcendentals=0),
    )(section, replica, delta, *[in_vmem(v) for v in (gain, wd, wu, *state)])
    return out[0], out[1:]


def backward_kernel(t, last, came, goes, section, replica, dy_in, gain, wdt, wut, x_all, z_all, r_all, *rest):
    s, q = section[0], replica[0]
    if len(rest) > 3:
        a_all, g_all, dyz_old, at_old, gt_old, dx_out, dyz, at, gt = rest
    else:
        dyz_old, dx_out, dyz = rest
    m = t - 2 * (last - s)
    micro, seq, width = x_all.shape
    replicas = dyz.shape[0]
    share = width // replicas
    cols = [(d, slice(d * share, (d + 1) * share)) for d in range(replicas)]
    busy = (m >= 0) & (m < micro)
    if len(rest) > 3:
        exchange(came, goes, s, q, dy_in, dx_out, a_all, g_all, at, gt)

    @pl.when(busy)
    def _():
        dg = None
        for d, c in cols:
            dy = dy_in[:, c]
            if t < micro:
                dy = jnp.where(s == last, dyz[d, m, :, :share], dy)
            dyz[d, m, :, :share] = dy
            part = nn(dy, wut[c, :])
            dg = part if dg is None else dg + part
        z = z_all[m]
        sig = sigmoid(z)
        dz = (dg * sig * (1.0 + z * (1.0 - sig))).astype(bf16)
        for d, c in cols:
            dyz[d, m, :, share:] = dz

        @pl.when(s > 0)
        def _():
            r = r_all[m][:, :1]
            coef = r * r * (jnp.sum(dz.astype(f32) * z, -1, keepdims=True) / width)
            for d, c in cols:
                u = nn(dz, wdt[:, c]) * gain[:, c]
                dx = dyz[d, m, :, :share].astype(f32) + r * u - x_all[m, :, c].astype(f32) * coef
                dx_out[:, c] = dx.astype(bf16)


def backward_step(t, last, came, goes, section, replica, dy, fixed, state):
    gain, wdt, wut, x_all = fixed[:4]
    micro, seq, width = x_all.shape
    rank = wdt.shape[0]
    out = pl.pallas_call(
        lambda *refs: backward_kernel(t, last, came, goes, *refs),
        name="backward",
        compiler_params=PARAMS,
        out_shape=[jax.ShapeDtypeStruct((seq, width), bf16)] + [VMEM(v.shape, v.dtype) for v in state],
        in_specs=[smem_spec()] * 2 + [vmem_spec()] * (1 + len(fixed) + len(state)),
        out_specs=[vmem_spec()] * (1 + len(state)),
        input_output_aliases={3 + len(fixed) + i: 1 + i for i in range(len(state))},
        cost_estimate=pl.CostEstimate(flops=4 * seq * width * rank, bytes_accessed=2 ** 20, transcendentals=0),
    )(section, replica, dy, *[in_vmem(v) for v in fixed], *[in_vmem(v) for v in state])
    return out[0], out[1:]


def keep_kernel(owner, anchors, x_all, kept, held, arrive, leave):
    slots = kept.shape[1]
    for j in range(slots):
        @pl.when(owner[j] >= 0)
        def _():
            pltpu.make_async_copy(x_all.at[owner[j]], held.at[j], arrive.at[j]).start()

        @pl.when(owner[j] < 0)
        def _():
            pltpu.make_async_copy(anchors.at[0, 0, j], held.at[j], arrive.at[j]).start()
    out = [pltpu.make_async_copy(held.at[j], kept.at[0, j], leave.at[j]) for j in range(slots)]
    for j in range(slots):
        pltpu.make_async_copy(anchors.at[0, 0, j], held.at[j], arrive.at[j]).wait()
        out[j].start()
    for copy in out:
        copy.wait()


def keep(owner, anchors, x_all):
    slots, seq, width = anchors.shape[2:]
    return pl.pallas_call(
        keep_kernel,
        name="keep",
        compiler_params=pltpu.CompilerParams(vmem_limit_bytes=8 * 2 ** 20),
        out_shape=pltpu.HBM((1, slots, seq, width), bf16),
        in_specs=[smem_spec(), hbm_spec(), hbm_spec()],
        out_specs=hbm_spec(),
        scratch_shapes=[VMEM((slots, seq, width), bf16)] + [pltpu.SemaphoreType.DMA((slots,))] * 2,
    )(owner, in_hbm(anchors), in_hbm(x_all))


def pack_kernel(dyz, out, sems):
    copies = [pltpu.make_async_copy(dyz.at[d], out.at[d], sems.at[d]) for d in range(dyz.shape[0])]
    for c in copies:
        c.start()
    for c in copies:
        c.wait()


def pack(dyz):
    return pl.pallas_call(
        pack_kernel,
        name="pack",
        compiler_params=PARAMS,
        out_shape=pltpu.HBM(dyz.shape, bf16),
        in_specs=[vmem_spec()],
        out_specs=hbm_spec(),
        scratch_shapes=[pltpu.SemaphoreType.DMA((dyz.shape[0],))],
    )(in_vmem(dyz))


def gradients_kernel(at, gt, dyz, down, up):
    share = at.shape[0]
    rank = gt.shape[0]
    block = 512

    def down_rows(i, _):
        part = pl.ds(pl.multiple_of(i * block, block), block)
        down[part, :] = nn(at[part, :], dyz[:, share:]).astype(bf16)
        return 0

    def up_rows(i, _):
        part = pl.ds(pl.multiple_of(i * block, block), block)
        up[part, :] = nn(gt[part, :], dyz[:, :share]).astype(bf16)
        return 0

    lax.fori_loop(0, share // block, down_rows, 0)
    lax.fori_loop(0, rank // block, up_rows, 0)


def gradients(at, gt, dyz):
    share, rows = at.shape
    rank = gt.shape[0]
    return pl.pallas_call(
        gradients_kernel,
        name="gradients",
        compiler_params=pltpu.CompilerParams(vmem_limit_bytes=24 * 2 ** 20),
        out_shape=[jax.ShapeDtypeStruct((share, rank), bf16), jax.ShapeDtypeStruct((rank, share), bf16)],
        in_specs=[vmem_spec()] * 3,
        out_specs=[vmem_spec()] * 2,
    )(in_vmem(at), in_vmem(gt), dyz)


def hops(t, last, steps, micro):
    final = (steps - 1) // 2 - 2
    k = t // 2
    low = 0 if k < 3 else min((k - 1) // 2 * 2 + 1, final - 2)
    high = low + 2 if low == 0 or low + 2 >= final else low + 1
    return low, [s for s in range(max(0, low - micro // 2 + 1), min(last - 1, high) + 1)]


def ride(last, steps, micro, replicas):
    groups = [hops(t, last, steps, micro) for t in range(steps - 2)]
    lows = list(dict.fromkeys(low for low, _ in groups))
    first = {low: min(t for t, g in enumerate(groups) if g[0] == low) for low in lows}
    final = {low: max(t for t, g in enumerate(groups) if g[0] == low) for low in lows}
    routes = []
    for back in (False, True):
        def at(s, back=back):
            return last - s if back else s
        routes.append([[(at(s), at(s + 1)) for s in senders] for _, senders in groups])

    def free(back, s):
        return [(back, low, parity) for low in lows for parity in (0, 1)
                if all(s not in pair for pair in routes[back][first[low]])]

    chosen = []
    for s in range(last + 1):
        done = [v for v in free(0, s) if first[v[1]] >= 2 * s + micro]
        late = [v for v in free(1, s) if first[v[1]] >= 2 * (last - s) + micro]
        early = [v for v in free(1, s) if final[v[1]] <= 2 * (last - s) - 3]
        order = [v for v in done if v[1] != lows[-1]] + [v for v in late if v[1] != lows[-1]]
        order += [v for v in done if v[1] == lows[-1]] + early + [v for v in late if v[1] == lows[-1]]
        chosen.append({v: [i + 1, 0] for i, v in enumerate(order[:replicas - 1])})
    plans = []
    for back in (0, 1):
        pairs, kinds = [], []
        for t in range(steps):
            kind = [0] * (last + 1)
            perm = []
            if t < steps - 2:
                for i, j in routes[back][t]:
                    perm += [(i * replicas + q, j * replicas + q) for q in range(replicas)]
                for s in range(last + 1):
                    slot = chosen[s].get((back, groups[t][0], t % 2))
                    if slot:
                        perm += [(s * replicas + q, s * replicas + (q + slot[0]) % replicas) for q in range(replicas)]
                        if slot[1] < 2:
                            slot[1] += 1
                            kind[s] = 4 * slot[0] + slot[1]
            pairs.append(perm)
            kinds.append(kind)
        plans.append((pairs, kinds))
    for s in range(last + 1):
        assert sorted(v[0] for v in chosen[s].values()) == list(range(1, replicas))
        assert all(v[1] == 2 for v in chosen[s].values())
        kinds = plans[1][1]
        idle = [t for t in range(steps) if kinds[t][s] == 0 and not 0 <= t - 2 * (last - s) < micro]
        kinds[idle[0]][s] = 3
    return plans


def shards(anchors, sample_ids, gain, w_down, w_up):
    section = jnp.full((1,), lax.axis_index("section"), jnp.int32)
    replica = jnp.full((1,), lax.axis_index("dp"), jnp.int32)
    sections = lax.axis_size("section")
    replicas = lax.axis_size("dp")
    slots = sample_ids[0]
    micro = slots.shape[0]
    store, seq, width = anchors.shape[2:]
    rank = w_down.shape[2]
    last = sections - 1
    steps = micro + 2 * last
    rows = micro * seq
    share = width // replicas
    (forth, forth_kinds), (back, back_kinds) = ride(last, steps, micro, replicas)
    none = [0] * sections
    match = slots[None, :] == jnp.arange(store, dtype=jnp.int32)[:, None]
    owner = jnp.max(jnp.where(match, jnp.arange(micro, dtype=jnp.int32)[None, :], -1), 1).astype(jnp.int32)
    nothing = jnp.zeros((seq, width), bf16)
    slots, owner, nothing = lax.optimization_barrier((slots, owner, nothing))

    gv, x_all, dyz, *rooms = load(
        section, replica, slots, anchors, gain,
        ((micro, seq, width), bf16),
        ((replicas, micro, seq, share + rank), bf16),
        [
            ((micro, seq, rank), f32),
            ((micro, seq, 128), f32),
            ((micro, seq, width), bf16),
            ((micro, seq, rank), bf16),
            ((rank, width), bf16),
            ((width, rank), bf16),
            ((share, replicas * rows), bf16),
            ((rank, replicas * rows), bf16),
        ])
    state = [x_all, *rooms[:4], dyz, *rooms[4:]]
    wd, wu = load_weights(gv, w_down, w_up)
    arrived = [nothing, nothing]
    for t in range(steps):
        came = forth_kinds[t - 2] if t >= 2 else none
        delta, state = forward_step(
            t, last, came, forth_kinds[t], section, replica, arrived[t], gv, wd, wu, state)
        if t < steps - 2:
            arrived.append(lax.ppermute(delta, ("section", "dp"), forth[t]))
    x_all, z_all, r_all, a_all, g_all, dyz, wdt, wut, at, gt = state

    state = [dyz, at, gt]
    fixed = [gv, wdt, wut, x_all, z_all, r_all, a_all, g_all]
    arrived = [nothing, nothing]
    filled = max(t for t in range(steps) if any(back_kinds[t])) + 2
    for t in range(steps):
        came = back_kinds[t - 2] if t >= 2 else none
        if t == filled + 1:
            at, gt = state[1:]
            fixed, state = fixed[:6], state[:1]
        dx, state = backward_step(t, last, came, back_kinds[t], section, replica, arrived[t], fixed, state)
        if t < steps - 2:
            arrived.append(lax.ppermute(dx, ("section", "dp"), back[t]))
    dyz, = state
    dyz, x_all = lax.optimization_barrier((pack(dyz), x_all))
    kept = keep(owner, anchors, x_all)
    dyz = lax.all_to_all(dyz, "dp", 0, 0, tiled=True).reshape(replicas * rows, share + rank)
    grad_down, grad_up = gradients(at, gt, dyz)
    return kept, grad_down[None], grad_up[None]


def solution(mesh):
    placed = (
        P("section", None, "dp", None, None),
        P("dp", None),
        P("section", None),
        P("section", None, None),
        P("section", None, None),
    )
    return jax.shard_map(
        shards,
        mesh=mesh,
        in_specs=placed,
        out_specs=(
            P("section", "dp", None, None),
            P("section", "dp", None),
            P("section", None, "dp"),
        ),
        check_vma=False,
    )
```

```python
import jax
import jax.numpy as jnp
from jax import lax
from jax.experimental import pallas as pl
from jax.experimental.pallas import tpu as pltpu
from jax.sharding import PartitionSpec as P

bf16 = jnp.bfloat16
f32 = jnp.float32
VMEM = pltpu.VMEM
PARAMS = pltpu.CompilerParams(vmem_limit_bytes=2 * 2 ** 20)
TASKS = 16


def vmem_spec():
    return pl.BlockSpec(memory_space=VMEM)


def smem_spec():
    return pl.BlockSpec(memory_space=pltpu.SMEM)


def hbm_spec():
    return pl.BlockSpec(memory_space=pltpu.HBM)


def in_vmem(x):
    return pltpu.with_memory_space_constraint(x, VMEM)


def in_hbm(x):
    return pltpu.with_memory_space_constraint(x, pltpu.HBM)


def nn(a, w):
    return lax.dot_general(a, w, (((1,), (0,)), ((), ())), preferred_element_type=f32)


def sigmoid(z):
    return 1.0 / (1.0 + jnp.exp(-z))


def idle_task(t, start, micro):
    return jnp.where(t < start, t, t - micro)


def load_kernel(section, replica, slots, anchors, gain, gv, x_all, dyz, *rest):
    sems = rest[-1]
    micro = x_all.shape[0]
    replicas = dyz.shape[0]
    share = x_all.shape[2] // replicas
    copies = [pltpu.make_async_copy(gain, gv, sems.at[0])]
    for m in range(micro):
        copies.append(pltpu.make_async_copy(anchors.at[0, 0, slots[m]], x_all.at[m], sems.at[1 + m]))
        for d in range(replicas):
            copies.append(pltpu.make_async_copy(
                anchors.at[0, 1, slots[m], :, pl.ds(d * share, share)],
                dyz.at[d, m, :, pl.ds(0, share)],
                sems.at[1 + micro + m * replicas + d]))
    for c in copies:
        c.start()
    for c in copies:
        c.wait()


def load(section, replica, slots, anchors, gain, x_all, dyz, rooms):
    micro = slots.shape[0]
    width = anchors.shape[4]
    shapes = [VMEM((1, width), f32)] + [VMEM(shape, dtype) for shape, dtype in (x_all, dyz, *rooms)]
    return pl.pallas_call(
        load_kernel,
        name="load",
        compiler_params=PARAMS,
        out_shape=shapes,
        in_specs=[smem_spec()] * 3 + [hbm_spec()] * 2,
        out_specs=[vmem_spec()] * len(shapes),
        scratch_shapes=[pltpu.SemaphoreType.DMA((1 + micro + micro * dyz[0][0],))],
    )(section, replica, slots, *[in_hbm(v) for v in (anchors, gain)])


def of_section(values, s):
    found = jnp.int32(0)
    for i, v in enumerate(values):
        if v:
            found = jnp.where(s == i, jnp.int32(v), found)
    return found


def exchange(came, goes, s, q, arrived, out, a_all, g_all, at, gt):
    micro = a_all.shape[0]
    share, total = at.shape
    rank = gt.shape[0]
    rows = micro * a_all.shape[1]
    replicas = total // rows

    def share_of(d):
        return pl.ds(pl.multiple_of(d * share, share), share)

    def rows_of(d):
        return pl.ds(pl.multiple_of(d * rows, rows), rows)

    if any(came):
        code = of_section(came, s)
        source = lax.rem(q + replicas - code // 4, replicas)

        @pl.when(code % 4 == 1)
        def _():
            block = jnp.concatenate([arrived[:, i * share:(i + 1) * share] for i in range(micro)], 0)
            at[:, rows_of(source)] = block.T

        @pl.when(code % 4 == 2)
        def _():
            block = jnp.concatenate([arrived[:, i * rank:(i + 1) * rank] for i in range(micro)], 0)
            gt[:, rows_of(source)] = block.T

    if any(goes):
        send = of_section(goes, s)
        target = lax.rem(q + send // 4, replicas)

        @pl.when(send % 4 == 1)
        def _():
            for i in range(micro):
                out[:, i * share:(i + 1) * share] = a_all[i, :, share_of(target)]

        @pl.when(send % 4 == 2)
        def _():
            for i in range(micro):
                out[:, i * rank:(i + 1) * rank] = g_all[i]

        if any(v == 3 for v in goes):
            @pl.when(send == 3)
            def _():
                at[:, rows_of(q)] = jnp.concatenate([a_all[i, :, share_of(q)] for i in range(micro)], 0).T
                gt[:, rows_of(q)] = jnp.concatenate([g_all[i] for i in range(micro)], 0).T


def load_weights_kernel(place, w_down, w_up, wd, wu, sems):
    copies = [
        pltpu.make_async_copy(w_down.at[0], wd, sems.at[0]),
        pltpu.make_async_copy(w_up.at[0], wu, sems.at[1]),
    ]
    for c in copies:
        c.start()
    for c in copies:
        c.wait()


def load_weights(gv, w_down, w_up):
    return pl.pallas_call(
        load_weights_kernel,
        name="weights",
        compiler_params=PARAMS,
        out_shape=[VMEM(w_down.shape[1:], bf16), VMEM(w_up.shape[1:], bf16)],
        in_specs=[vmem_spec(), hbm_spec(), hbm_spec()],
        out_specs=[vmem_spec()] * 2,
        scratch_shapes=[pltpu.SemaphoreType.DMA((2,))],
    )(in_vmem(gv), in_hbm(w_down), in_hbm(w_up))


def forward_kernel(t, last, came, goes, section, replica, delta_in, gain, wd, wu,
                   x_old, z_old, r_old, a_old, g_old, dyz_old, wdt_old, wut_old, at_old, gt_old,
                   delta_out, x_all, z_all, r_all, a_all, g_all, dyz, wdt, wut, at, gt):
    s, q = section[0], replica[0]
    m = t - 2 * s
    micro, seq, width = x_all.shape
    rank = wd.shape[1]
    share = width // dyz.shape[0]
    cols = [(d, slice(d * share, (d + 1) * share)) for d in range(dyz.shape[0])]
    busy = (m >= 0) & (m < micro)
    task = idle_task(t, 2 * s, micro)
    exchange(came, goes, s, q, delta_in, delta_out, a_all, g_all, at, gt)

    @pl.when(jnp.logical_not(busy) & (task < TASKS))
    def _():
        step = width // TASKS
        part = pl.ds(pl.multiple_of(task * step, step), step)
        wut[part, :] = wu[:, part].T
        wdt[:, part] = wd[part, :].T

    @pl.when(busy)
    def _():
        total = jnp.zeros((seq, 128), f32)
        for d, c in cols:
            x = (x_all[m, :, c].astype(f32) + delta_in[:, c].astype(f32)).astype(bf16)
            x_all[m, :, c] = x
            h = x.astype(f32)
            sq = h * h
            for k in range(0, share, 128):
                total = total + sq[:, k:k + 128]
        r = lax.rsqrt(jnp.sum(total, -1, keepdims=True) / width + 1e-05)
        r_all[m] = jnp.broadcast_to(r, (seq, 128))
        z = None
        for d, c in cols:
            a = (x_all[m, :, c].astype(f32) * r * gain[:, c]).astype(bf16)
            a_all[m, :, c] = a
            part = nn(a, wd[c, :])
            z = part if z is None else z + part
        z_all[m] = z
        g = (z * sigmoid(z)).astype(bf16)
        g_all[m] = g
        for d, c in cols:
            y = (x_all[m, :, c].astype(f32) + nn(g, wu[:, c])).astype(bf16)
            delta_out[:, c] = (y.astype(f32) - dyz[d, m, :, :share].astype(f32)).astype(bf16)

        @pl.when(s == last)
        def _():
            for d, c in cols:
                dyz[d, m, :, :share] = delta_out[:, c]


def forward_step(t, last, came, goes, section, replica, delta, gain, wd, wu, state):
    micro, seq, width = state[0].shape
    rank = wd.shape[1]
    out = pl.pallas_call(
        lambda *refs: forward_kernel(t, last, came, goes, *refs),
        name="forward",
        compiler_params=PARAMS,
        out_shape=[jax.ShapeDtypeStruct((seq, width), bf16)] + [VMEM(v.shape, v.dtype) for v in state],
        in_specs=[smem_spec()] * 2 + [vmem_spec()] * (4 + len(state)),
        out_specs=[vmem_spec()] * (1 + len(state)),
        input_output_aliases={6 + i: 1 + i for i in range(len(state))},
        cost_estimate=pl.CostEstimate(flops=4 * seq * width * rank, bytes_accessed=2 ** 20, transcendentals=0),
    )(section, replica, delta, *[in_vmem(v) for v in (gain, wd, wu, *state)])
    return out[0], out[1:]


def backward_kernel(t, last, came, goes, section, replica, dy_in, gain, wdt, wut, x_all, z_all, r_all, *rest):
    s, q = section[0], replica[0]
    if len(rest) > 3:
        a_all, g_all, dyz_old, at_old, gt_old, dx_out, dyz, at, gt = rest
    else:
        dyz_old, dx_out, dyz = rest
    m = t - 2 * (last - s)
    micro, seq, width = x_all.shape
    replicas = dyz.shape[0]
    share = width // replicas
    cols = [(d, slice(d * share, (d + 1) * share)) for d in range(replicas)]
    busy = (m >= 0) & (m < micro)
    if len(rest) > 3:
        exchange(came, goes, s, q, dy_in, dx_out, a_all, g_all, at, gt)

    @pl.when(busy)
    def _():
        dg = None
        for d, c in cols:
            dy = dy_in[:, c]
            if t < micro:
                dy = jnp.where(s == last, dyz[d, m, :, :share], dy)
            dyz[d, m, :, :share] = dy
            part = nn(dy, wut[c, :])
            dg = part if dg is None else dg + part
        z = z_all[m]
        sig = sigmoid(z)
        dz = (dg * sig * (1.0 + z * (1.0 - sig))).astype(bf16)
        for d, c in cols:
            dyz[d, m, :, share:] = dz

        @pl.when(s > 0)
        def _():
            r = r_all[m][:, :1]
            coef = r * r * (jnp.sum(dz.astype(f32) * z, -1, keepdims=True) / width)
            for d, c in cols:
                u = nn(dz, wdt[:, c]) * gain[:, c]
                dx = dyz[d, m, :, :share].astype(f32) + r * u - x_all[m, :, c].astype(f32) * coef
                dx_out[:, c] = dx.astype(bf16)


def backward_step(t, last, came, goes, section, replica, dy, fixed, state):
    gain, wdt, wut, x_all = fixed[:4]
    micro, seq, width = x_all.shape
    rank = wdt.shape[0]
    out = pl.pallas_call(
        lambda *refs: backward_kernel(t, last, came, goes, *refs),
        name="backward",
        compiler_params=PARAMS,
        out_shape=[jax.ShapeDtypeStruct((seq, width), bf16)] + [VMEM(v.shape, v.dtype) for v in state],
        in_specs=[smem_spec()] * 2 + [vmem_spec()] * (1 + len(fixed) + len(state)),
        out_specs=[vmem_spec()] * (1 + len(state)),
        input_output_aliases={3 + len(fixed) + i: 1 + i for i in range(len(state))},
        cost_estimate=pl.CostEstimate(flops=4 * seq * width * rank, bytes_accessed=2 ** 20, transcendentals=0),
    )(section, replica, dy, *[in_vmem(v) for v in fixed], *[in_vmem(v) for v in state])
    return out[0], out[1:]


def keep_kernel(owner, anchors, x_all, kept, held, arrive, leave):
    slots = kept.shape[1]
    for j in range(slots):
        @pl.when(owner[j] >= 0)
        def _():
            pltpu.make_async_copy(x_all.at[owner[j]], held.at[j], arrive.at[j]).start()

        @pl.when(owner[j] < 0)
        def _():
            pltpu.make_async_copy(anchors.at[0, 0, j], held.at[j], arrive.at[j]).start()
    out = [pltpu.make_async_copy(held.at[j], kept.at[0, j], leave.at[j]) for j in range(slots)]
    for j in range(slots):
        pltpu.make_async_copy(anchors.at[0, 0, j], held.at[j], arrive.at[j]).wait()
        out[j].start()
    for copy in out:
        copy.wait()


def keep(owner, anchors, x_all):
    slots, seq, width = anchors.shape[2:]
    return pl.pallas_call(
        keep_kernel,
        name="keep",
        compiler_params=pltpu.CompilerParams(vmem_limit_bytes=8 * 2 ** 20),
        out_shape=pltpu.HBM((1, slots, seq, width), bf16),
        in_specs=[smem_spec(), hbm_spec(), hbm_spec()],
        out_specs=hbm_spec(),
        scratch_shapes=[VMEM((slots, seq, width), bf16)] + [pltpu.SemaphoreType.DMA((slots,))] * 2,
    )(owner, in_hbm(anchors), in_hbm(x_all))


def pack_kernel(dyz, out, sems):
    copies = [pltpu.make_async_copy(dyz.at[d], out.at[d], sems.at[d]) for d in range(dyz.shape[0])]
    for c in copies:
        c.start()
    for c in copies:
        c.wait()


def pack(dyz):
    return pl.pallas_call(
        pack_kernel,
        name="pack",
        compiler_params=PARAMS,
        out_shape=pltpu.HBM(dyz.shape, bf16),
        in_specs=[vmem_spec()],
        out_specs=hbm_spec(),
        scratch_shapes=[pltpu.SemaphoreType.DMA((dyz.shape[0],))],
    )(in_vmem(dyz))


def gradients_kernel(at, gt, dyz, down, up):
    share = at.shape[0]
    rank = gt.shape[0]
    block = 512

    def down_rows(i, _):
        part = pl.ds(pl.multiple_of(i * block, block), block)
        down[part, :] = nn(at[part, :], dyz[:, share:]).astype(bf16)
        return 0

    def up_rows(i, _):
        part = pl.ds(pl.multiple_of(i * block, block), block)
        up[part, :] = nn(gt[part, :], dyz[:, :share]).astype(bf16)
        return 0

    lax.fori_loop(0, share // block, down_rows, 0)
    lax.fori_loop(0, rank // block, up_rows, 0)


def gradients(at, gt, dyz):
    share, rows = at.shape
    rank = gt.shape[0]
    return pl.pallas_call(
        gradients_kernel,
        name="gradients",
        compiler_params=pltpu.CompilerParams(vmem_limit_bytes=24 * 2 ** 20),
        out_shape=[jax.ShapeDtypeStruct((share, rank), bf16), jax.ShapeDtypeStruct((rank, share), bf16)],
        in_specs=[vmem_spec()] * 3,
        out_specs=[vmem_spec()] * 2,
    )(in_vmem(at), in_vmem(gt), dyz)


def hops(t, last, steps, micro):
    final = (steps - 1) // 2 - 2
    k = t // 2
    low = 0 if k < 3 else min((k - 1) // 2 * 2 + 1, final - 1)
    high = low + 2 if low == 0 or low + 2 >= final else low + 1
    return low, [s for s in range(max(0, low - micro // 2 + 1), min(last - 1, high) + 1)]


def ride(last, steps, micro, replicas):
    groups = [hops(t, last, steps, micro) for t in range(steps - 2)]
    lows = list(dict.fromkeys(low for low, _ in groups))
    first = {low: min(t for t, g in enumerate(groups) if g[0] == low) for low in lows}
    final = {low: max(t for t, g in enumerate(groups) if g[0] == low) for low in lows}
    routes = []
    for back in (False, True):
        def at(s, back=back):
            return last - s if back else s
        routes.append([[(at(s), at(s + 1)) for s in senders] for _, senders in groups])

    def free(back, s):
        return [(back, low, parity) for low in lows for parity in (0, 1)
                if all(s not in pair for pair in routes[back][first[low]])]

    chosen = []
    for s in range(last + 1):
        done = [v for v in free(0, s) if first[v[1]] >= 2 * s + micro]
        late = [v for v in free(1, s) if first[v[1]] >= 2 * (last - s) + micro]
        early = [v for v in free(1, s) if final[v[1]] <= 2 * (last - s) - 3]
        order = [v for v in done if v[1] != lows[-1]] + [v for v in late if v[1] != lows[-1]]
        order += [v for v in done if v[1] == lows[-1]] + early + [v for v in late if v[1] == lows[-1]]
        chosen.append({v: [i + 1, 0] for i, v in enumerate(order[:replicas - 1])})
    plans = []
    for back in (0, 1):
        pairs, kinds = [], []
        for t in range(steps):
            kind = [0] * (last + 1)
            perm = []
            if t < steps - 2:
                for i, j in routes[back][t]:
                    perm += [(i * replicas + q, j * replicas + q) for q in range(replicas)]
                for s in range(last + 1):
                    slot = chosen[s].get((back, groups[t][0], t % 2))
                    if slot:
                        perm += [(s * replicas + q, s * replicas + (q + slot[0]) % replicas) for q in range(replicas)]
                        if slot[1] < 2:
                            slot[1] += 1
                            kind[s] = 4 * slot[0] + slot[1]
            pairs.append(perm)
            kinds.append(kind)
        plans.append((pairs, kinds))
    for s in range(last + 1):
        assert sorted(v[0] for v in chosen[s].values()) == list(range(1, replicas))
        assert all(v[1] == 2 for v in chosen[s].values())
        kinds = plans[1][1]
        idle = [t for t in range(steps) if kinds[t][s] == 0 and not 0 <= t - 2 * (last - s) < micro]
        kinds[idle[0]][s] = 3
    return plans


def shards(anchors, sample_ids, gain, w_down, w_up):
    section = jnp.full((1,), lax.axis_index("section"), jnp.int32)
    replica = jnp.full((1,), lax.axis_index("dp"), jnp.int32)
    sections = lax.axis_size("section")
    replicas = lax.axis_size("dp")
    slots = sample_ids[0]
    micro = slots.shape[0]
    store, seq, width = anchors.shape[2:]
    rank = w_down.shape[2]
    last = sections - 1
    steps = micro + 2 * last
    rows = micro * seq
    share = width // replicas
    (forth, forth_kinds), (back, back_kinds) = ride(last, steps, micro, replicas)
    none = [0] * sections
    match = slots[None, :] == jnp.arange(store, dtype=jnp.int32)[:, None]
    owner = jnp.max(jnp.where(match, jnp.arange(micro, dtype=jnp.int32)[None, :], -1), 1).astype(jnp.int32)
    nothing = jnp.zeros((seq, width), bf16)
    slots, owner, nothing = lax.optimization_barrier((slots, owner, nothing))

    gv, x_all, dyz, *rooms = load(
        section, replica, slots, anchors, gain,
        ((micro, seq, width), bf16),
        ((replicas, micro, seq, share + rank), bf16),
        [
            ((micro, seq, rank), f32),
            ((micro, seq, 128), f32),
            ((micro, seq, width), bf16),
            ((micro, seq, rank), bf16),
            ((rank, width), bf16),
            ((width, rank), bf16),
            ((share, replicas * rows), bf16),
            ((rank, replicas * rows), bf16),
        ])
    state = [x_all, *rooms[:4], dyz, *rooms[4:]]
    wd, wu = load_weights(gv, w_down, w_up)
    arrived = [nothing, nothing]
    for t in range(steps):
        came = forth_kinds[t - 2] if t >= 2 else none
        delta, state = forward_step(
            t, last, came, forth_kinds[t], section, replica, arrived[t], gv, wd, wu, state)
        if t < steps - 2:
            arrived.append(lax.ppermute(delta, ("section", "dp"), forth[t]))
    x_all, z_all, r_all, a_all, g_all, dyz, wdt, wut, at, gt = state

    state = [dyz, at, gt]
    fixed = [gv, wdt, wut, x_all, z_all, r_all, a_all, g_all]
    arrived = [nothing, nothing]
    filled = max(t for t in range(steps) if any(back_kinds[t])) + 2
    for t in range(steps):
        came = back_kinds[t - 2] if t >= 2 else none
        if t == filled + 1:
            at, gt = state[1:]
            fixed, state = fixed[:6], state[:1]
        dx, state = backward_step(t, last, came, back_kinds[t], section, replica, arrived[t], fixed, state)
        if t < steps - 2:
            arrived.append(lax.ppermute(dx, ("section", "dp"), back[t]))
    dyz, = state
    dyz, x_all = lax.optimization_barrier((pack(dyz), x_all))
    kept = keep(owner, anchors, x_all)
    dyz = lax.all_to_all(dyz, "dp", 0, 0, tiled=True).reshape(replicas * rows, share + rank)
    grad_down, grad_up = gradients(at, gt, dyz)
    return kept, grad_down[None], grad_up[None]


def solution(mesh):
    placed = (
        P("section", None, "dp", None, None),
        P("dp", None),
        P("section", None),
        P("section", None, None),
        P("section", None, None),
    )
    return jax.shard_map(
        shards,
        mesh=mesh,
        in_specs=placed,
        out_specs=(
            P("section", "dp", None, None),
            P("section", "dp", None),
            P("section", None, "dp"),
        ),
        check_vma=False,
    )
```

```python
import jax
import jax.numpy as jnp
from jax import lax
from jax.experimental import pallas as pl
from jax.experimental.pallas import tpu as pltpu
from jax.sharding import PartitionSpec as P

bf16 = jnp.bfloat16
f32 = jnp.float32
VMEM = pltpu.VMEM
PARAMS = pltpu.CompilerParams(vmem_limit_bytes=2 * 2 ** 20)
TASKS = 16


def vmem_spec():
    return pl.BlockSpec(memory_space=VMEM)


def smem_spec():
    return pl.BlockSpec(memory_space=pltpu.SMEM)


def hbm_spec():
    return pl.BlockSpec(memory_space=pltpu.HBM)


def in_vmem(x):
    return pltpu.with_memory_space_constraint(x, VMEM)


def in_hbm(x):
    return pltpu.with_memory_space_constraint(x, pltpu.HBM)


def nn(a, w):
    return lax.dot_general(a, w, (((1,), (0,)), ((), ())), preferred_element_type=f32)


def sigmoid(z):
    return 1.0 / (1.0 + jnp.exp(-z))


def idle_task(t, start, micro):
    return jnp.where(t < start, t, t - micro)


def load_kernel(section, replica, slots, anchors, gain, w_down, w_up, wd, wu, gv, x_all, dyz, *rest):
    sems = rest[-1]
    micro = x_all.shape[0]
    replicas = dyz.shape[0]
    share = x_all.shape[2] // replicas
    copies = [
        pltpu.make_async_copy(w_down.at[0], wd, sems.at[1]),
        pltpu.make_async_copy(gain, gv, sems.at[0]),
    ]
    for m in range(micro):
        copies.append(pltpu.make_async_copy(anchors.at[0, 0, slots[m]], x_all.at[m], sems.at[3 + m]))
        for d in range(replicas):
            copies.append(pltpu.make_async_copy(
                anchors.at[0, 1, slots[m], :, pl.ds(d * share, share)],
                dyz.at[d, m, :, pl.ds(0, share)],
                sems.at[3 + micro + m * replicas + d]))
    copies.append(pltpu.make_async_copy(w_up.at[0], wu, sems.at[2]))
    for c in copies:
        c.start()
    for c in copies:
        c.wait()


def load(section, replica, slots, anchors, gain, w_down, w_up, x_all, dyz, rooms):
    micro = slots.shape[0]
    width = anchors.shape[4]
    shapes = [VMEM(v.shape[1:], bf16) for v in (w_down, w_up)] + [VMEM((1, width), f32)] + [VMEM(shape, dtype) for shape, dtype in (x_all, dyz, *rooms)]
    return pl.pallas_call(
        load_kernel,
        name="load",
        compiler_params=PARAMS,
        out_shape=shapes,
        in_specs=[smem_spec()] * 3 + [hbm_spec()] * 4,
        out_specs=[vmem_spec()] * len(shapes),
        scratch_shapes=[pltpu.SemaphoreType.DMA((3 + micro + micro * dyz[0][0],))],
    )(section, replica, slots, *[in_hbm(v) for v in (anchors, gain, w_down, w_up)])


def of_section(values, s):
    found = jnp.int32(0)
    for i, v in enumerate(values):
        if v:
            found = jnp.where(s == i, jnp.int32(v), found)
    return found


def exchange(came, goes, s, q, arrived, out, a_all, g_all, at, gt):
    micro = a_all.shape[0]
    share, total = at.shape
    rank = gt.shape[0]
    rows = micro * a_all.shape[1]
    replicas = total // rows

    def share_of(d):
        return pl.ds(pl.multiple_of(d * share, share), share)

    def rows_of(d):
        return pl.ds(pl.multiple_of(d * rows, rows), rows)

    if any(came):
        code = of_section(came, s)
        source = lax.rem(q + replicas - code // 4, replicas)

        @pl.when(code % 4 == 1)
        def _():
            block = jnp.concatenate([arrived[:, i * share:(i + 1) * share] for i in range(micro)], 0)
            at[:, rows_of(source)] = block.T

        @pl.when(code % 4 == 2)
        def _():
            block = jnp.concatenate([arrived[:, i * rank:(i + 1) * rank] for i in range(micro)], 0)
            gt[:, rows_of(source)] = block.T

    if any(goes):
        send = of_section(goes, s)
        target = lax.rem(q + send // 4, replicas)

        @pl.when(send % 4 == 1)
        def _():
            for i in range(micro):
                out[:, i * share:(i + 1) * share] = a_all[i, :, share_of(target)]

        @pl.when(send % 4 == 2)
        def _():
            for i in range(micro):
                out[:, i * rank:(i + 1) * rank] = g_all[i]

        if any(v == 3 for v in goes):
            @pl.when(send == 3)
            def _():
                at[:, rows_of(q)] = jnp.concatenate([a_all[i, :, share_of(q)] for i in range(micro)], 0).T
                gt[:, rows_of(q)] = jnp.concatenate([g_all[i] for i in range(micro)], 0).T


def forward_kernel(t, last, came, goes, section, replica, delta_in, gain, wd, wu,
                   x_old, z_old, r_old, a_old, g_old, dyz_old, wdt_old, wut_old, at_old, gt_old,
                   delta_out, x_all, z_all, r_all, a_all, g_all, dyz, wdt, wut, at, gt):
    s, q = section[0], replica[0]
    m = t - 2 * s
    micro, seq, width = x_all.shape
    rank = wd.shape[1]
    share = width // dyz.shape[0]
    cols = [(d, slice(d * share, (d + 1) * share)) for d in range(dyz.shape[0])]
    busy = (m >= 0) & (m < micro)
    task = idle_task(t, 2 * s, micro)
    exchange(came, goes, s, q, delta_in, delta_out, a_all, g_all, at, gt)

    @pl.when(jnp.logical_not(busy) & (task < TASKS))
    def _():
        step = width // TASKS
        part = pl.ds(pl.multiple_of(task * step, step), step)
        wut[part, :] = wu[:, part].T
        wdt[:, part] = wd[part, :].T

    @pl.when(busy)
    def _():
        total = jnp.zeros((seq, 128), f32)
        for d, c in cols:
            x = (x_all[m, :, c].astype(f32) + delta_in[:, c].astype(f32)).astype(bf16)
            x_all[m, :, c] = x
            h = x.astype(f32)
            sq = h * h
            for k in range(0, share, 128):
                total = total + sq[:, k:k + 128]
        r = lax.rsqrt(jnp.sum(total, -1, keepdims=True) / width + 1e-05)
        r_all[m] = jnp.broadcast_to(r, (seq, 128))
        z = None
        for d, c in cols:
            a = (x_all[m, :, c].astype(f32) * r * gain[:, c]).astype(bf16)
            a_all[m, :, c] = a
            part = nn(a, wd[c, :])
            z = part if z is None else z + part
        z_all[m] = z
        g = (z * sigmoid(z)).astype(bf16)
        g_all[m] = g
        for d, c in cols:
            y = (x_all[m, :, c].astype(f32) + nn(g, wu[:, c])).astype(bf16)
            delta_out[:, c] = (y.astype(f32) - dyz[d, m, :, :share].astype(f32)).astype(bf16)

        @pl.when(s == last)
        def _():
            for d, c in cols:
                dyz[d, m, :, :share] = delta_out[:, c]


def forward_step(t, last, came, goes, section, replica, delta, gain, wd, wu, state):
    micro, seq, width = state[0].shape
    rank = wd.shape[1]
    out = pl.pallas_call(
        lambda *refs: forward_kernel(t, last, came, goes, *refs),
        name="forward",
        compiler_params=PARAMS,
        out_shape=[jax.ShapeDtypeStruct((seq, width), bf16)] + [VMEM(v.shape, v.dtype) for v in state],
        in_specs=[smem_spec()] * 2 + [vmem_spec()] * (4 + len(state)),
        out_specs=[vmem_spec()] * (1 + len(state)),
        input_output_aliases={6 + i: 1 + i for i in range(len(state))},
        cost_estimate=pl.CostEstimate(flops=4 * seq * width * rank, bytes_accessed=2 ** 20, transcendentals=0),
    )(section, replica, delta, *[in_vmem(v) for v in (gain, wd, wu, *state)])
    return out[0], out[1:]


def backward_kernel(t, last, came, goes, section, replica, dy_in, gain, wdt, wut, x_all, z_all, r_all, *rest):
    s, q = section[0], replica[0]
    if len(rest) > 3:
        a_all, g_all, dyz_old, at_old, gt_old, dx_out, dyz, at, gt = rest
    else:
        dyz_old, dx_out, dyz = rest
    m = t - 2 * (last - s)
    micro, seq, width = x_all.shape
    replicas = dyz.shape[0]
    share = width // replicas
    cols = [(d, slice(d * share, (d + 1) * share)) for d in range(replicas)]
    busy = (m >= 0) & (m < micro)
    if len(rest) > 3:
        exchange(came, goes, s, q, dy_in, dx_out, a_all, g_all, at, gt)

    @pl.when(busy)
    def _():
        dg = None
        for d, c in cols:
            dy = dy_in[:, c]
            if t < micro:
                dy = jnp.where(s == last, dyz[d, m, :, :share], dy)
            dyz[d, m, :, :share] = dy
            part = nn(dy, wut[c, :])
            dg = part if dg is None else dg + part
        z = z_all[m]
        sig = sigmoid(z)
        dz = (dg * sig * (1.0 + z * (1.0 - sig))).astype(bf16)
        for d, c in cols:
            dyz[d, m, :, share:] = dz

        @pl.when(s > 0)
        def _():
            r = r_all[m][:, :1]
            coef = r * r * (jnp.sum(dz.astype(f32) * z, -1, keepdims=True) / width)
            for d, c in cols:
                u = nn(dz, wdt[:, c]) * gain[:, c]
                dx = dyz[d, m, :, :share].astype(f32) + r * u - x_all[m, :, c].astype(f32) * coef
                dx_out[:, c] = dx.astype(bf16)


def backward_step(t, last, came, goes, section, replica, dy, fixed, state):
    gain, wdt, wut, x_all = fixed[:4]
    micro, seq, width = x_all.shape
    rank = wdt.shape[0]
    out = pl.pallas_call(
        lambda *refs: backward_kernel(t, last, came, goes, *refs),
        name="backward",
        compiler_params=PARAMS,
        out_shape=[jax.ShapeDtypeStruct((seq, width), bf16)] + [VMEM(v.shape, v.dtype) for v in state],
        in_specs=[smem_spec()] * 2 + [vmem_spec()] * (1 + len(fixed) + len(state)),
        out_specs=[vmem_spec()] * (1 + len(state)),
        input_output_aliases={3 + len(fixed) + i: 1 + i for i in range(len(state))},
        cost_estimate=pl.CostEstimate(flops=4 * seq * width * rank, bytes_accessed=2 ** 20, transcendentals=0),
    )(section, replica, dy, *[in_vmem(v) for v in fixed], *[in_vmem(v) for v in state])
    return out[0], out[1:]


def keep_kernel(owner, anchors, x_all, kept, held, arrive, leave):
    slots = kept.shape[1]
    for j in range(slots):
        @pl.when(owner[j] >= 0)
        def _():
            pltpu.make_async_copy(x_all.at[owner[j]], held.at[j], arrive.at[j]).start()

        @pl.when(owner[j] < 0)
        def _():
            pltpu.make_async_copy(anchors.at[0, 0, j], held.at[j], arrive.at[j]).start()
    out = [pltpu.make_async_copy(held.at[j], kept.at[0, j], leave.at[j]) for j in range(slots)]
    for j in range(slots):
        pltpu.make_async_copy(anchors.at[0, 0, j], held.at[j], arrive.at[j]).wait()
        out[j].start()
    for copy in out:
        copy.wait()


def keep(owner, anchors, x_all):
    slots, seq, width = anchors.shape[2:]
    return pl.pallas_call(
        keep_kernel,
        name="keep",
        compiler_params=pltpu.CompilerParams(vmem_limit_bytes=8 * 2 ** 20),
        out_shape=pltpu.HBM((1, slots, seq, width), bf16),
        in_specs=[smem_spec(), hbm_spec(), hbm_spec()],
        out_specs=hbm_spec(),
        scratch_shapes=[VMEM((slots, seq, width), bf16)] + [pltpu.SemaphoreType.DMA((slots,))] * 2,
    )(owner, in_hbm(anchors), in_hbm(x_all))


def pack_kernel(dyz, out, sems):
    copies = [pltpu.make_async_copy(dyz.at[d], out.at[d], sems.at[d]) for d in range(dyz.shape[0])]
    for c in copies:
        c.start()
    for c in copies:
        c.wait()


def pack(dyz):
    return pl.pallas_call(
        pack_kernel,
        name="pack",
        compiler_params=PARAMS,
        out_shape=pltpu.HBM(dyz.shape, bf16),
        in_specs=[vmem_spec()],
        out_specs=hbm_spec(),
        scratch_shapes=[pltpu.SemaphoreType.DMA((dyz.shape[0],))],
    )(in_vmem(dyz))


def gradients_kernel(at, gt, dyz, down, up):
    share = at.shape[0]
    rank = gt.shape[0]
    block = 512

    def down_rows(i, _):
        part = pl.ds(pl.multiple_of(i * block, block), block)
        down[part, :] = nn(at[part, :], dyz[:, share:]).astype(bf16)
        return 0

    def up_rows(i, _):
        part = pl.ds(pl.multiple_of(i * block, block), block)
        up[part, :] = nn(gt[part, :], dyz[:, :share]).astype(bf16)
        return 0

    lax.fori_loop(0, share // block, down_rows, 0)
    lax.fori_loop(0, rank // block, up_rows, 0)


def gradients(at, gt, dyz):
    share, rows = at.shape
    rank = gt.shape[0]
    return pl.pallas_call(
        gradients_kernel,
        name="gradients",
        compiler_params=pltpu.CompilerParams(vmem_limit_bytes=24 * 2 ** 20),
        out_shape=[jax.ShapeDtypeStruct((share, rank), bf16), jax.ShapeDtypeStruct((rank, share), bf16)],
        in_specs=[vmem_spec()] * 3,
        out_specs=[vmem_spec()] * 2,
    )(in_vmem(at), in_vmem(gt), dyz)


def hops(t, last, steps, micro):
    final = (steps - 1) // 2 - 2
    k = t // 2
    low = 0 if k < 3 else min((k - 1) // 2 * 2 + 1, final - 1)
    high = low + 2 if low == 0 or low + 2 >= final else low + 1
    return low, [s for s in range(max(0, low - micro // 2 + 1), min(last - 1, high) + 1)]


def ride(last, steps, micro, replicas):
    groups = [hops(t, last, steps, micro) for t in range(steps - 2)]
    lows = list(dict.fromkeys(low for low, _ in groups))
    first = {low: min(t for t, g in enumerate(groups) if g[0] == low) for low in lows}
    final = {low: max(t for t, g in enumerate(groups) if g[0] == low) for low in lows}
    routes = []
    for back in (False, True):
        def at(s, back=back):
            return last - s if back else s
        routes.append([[(at(s), at(s + 1)) for s in senders] for _, senders in groups])

    def free(back, s):
        return [(back, low, parity) for low in lows for parity in (0, 1)
                if all(s not in pair for pair in routes[back][first[low]])]

    chosen = []
    for s in range(last + 1):
        done = [v for v in free(0, s) if first[v[1]] >= 2 * s + micro]
        late = [v for v in free(1, s) if first[v[1]] >= 2 * (last - s) + micro]
        early = [v for v in free(1, s) if final[v[1]] <= 2 * (last - s) - 3]
        order = [v for v in done if v[1] != lows[-1]] + [v for v in late if v[1] != lows[-1]]
        order += [v for v in done if v[1] == lows[-1]] + early + [v for v in late if v[1] == lows[-1]]
        chosen.append({v: [i + 1, 0] for i, v in enumerate(order[:replicas - 1])})
    plans = []
    for back in (0, 1):
        pairs, kinds = [], []
        for t in range(steps):
            kind = [0] * (last + 1)
            perm = []
            if t < steps - 2:
                for i, j in routes[back][t]:
                    perm += [(i * replicas + q, j * replicas + q) for q in range(replicas)]
                for s in range(last + 1):
                    slot = chosen[s].get((back, groups[t][0], t % 2))
                    if slot:
                        perm += [(s * replicas + q, s * replicas + (q + slot[0]) % replicas) for q in range(replicas)]
                        if slot[1] < 2:
                            slot[1] += 1
                            kind[s] = 4 * slot[0] + slot[1]
            pairs.append(perm)
            kinds.append(kind)
        plans.append((pairs, kinds))
    for s in range(last + 1):
        assert sorted(v[0] for v in chosen[s].values()) == list(range(1, replicas))
        assert all(v[1] == 2 for v in chosen[s].values())
        kinds = plans[1][1]
        idle = [t for t in range(steps) if kinds[t][s] == 0 and not 0 <= t - 2 * (last - s) < micro]
        kinds[idle[0]][s] = 3
    return plans


def shards(anchors, sample_ids, gain, w_down, w_up):
    section = jnp.full((1,), lax.axis_index("section"), jnp.int32)
    replica = jnp.full((1,), lax.axis_index("dp"), jnp.int32)
    sections = lax.axis_size("section")
    replicas = lax.axis_size("dp")
    slots = sample_ids[0]
    micro = slots.shape[0]
    store, seq, width = anchors.shape[2:]
    rank = w_down.shape[2]
    last = sections - 1
    steps = micro + 2 * last
    rows = micro * seq
    share = width // replicas
    (forth, forth_kinds), (back, back_kinds) = ride(last, steps, micro, replicas)
    none = [0] * sections
    match = slots[None, :] == jnp.arange(store, dtype=jnp.int32)[:, None]
    owner = jnp.max(jnp.where(match, jnp.arange(micro, dtype=jnp.int32)[None, :], -1), 1).astype(jnp.int32)
    nothing = jnp.zeros((seq, width), bf16)
    slots, owner, nothing = lax.optimization_barrier((slots, owner, nothing))

    wd, wu, gv, x_all, dyz, *rooms = load(
        section, replica, slots, anchors, gain, w_down, w_up,
        ((micro, seq, width), bf16),
        ((replicas, micro, seq, share + rank), bf16),
        [
            ((micro, seq, rank), f32),
            ((micro, seq, 128), f32),
            ((micro, seq, width), bf16),
            ((micro, seq, rank), bf16),
            ((rank, width), bf16),
            ((width, rank), bf16),
            ((share, replicas * rows), bf16),
            ((rank, replicas * rows), bf16),
        ])
    state = [x_all, *rooms[:4], dyz, *rooms[4:]]
    arrived = [nothing, nothing]
    for t in range(steps):
        came = forth_kinds[t - 2] if t >= 2 else none
        delta, state = forward_step(
            t, last, came, forth_kinds[t], section, replica, arrived[t], gv, wd, wu, state)
        if t < steps - 2:
            arrived.append(lax.ppermute(delta, ("section", "dp"), forth[t]))
    x_all, z_all, r_all, a_all, g_all, dyz, wdt, wut, at, gt = state

    state = [dyz, at, gt]
    fixed = [gv, wdt, wut, x_all, z_all, r_all, a_all, g_all]
    arrived = [nothing, nothing]
    filled = max(t for t in range(steps) if any(back_kinds[t])) + 2
    for t in range(steps):
        came = back_kinds[t - 2] if t >= 2 else none
        if t == filled + 1:
            at, gt = state[1:]
            fixed, state = fixed[:6], state[:1]
        dx, state = backward_step(t, last, came, back_kinds[t], section, replica, arrived[t], fixed, state)
        if t < steps - 2:
            arrived.append(lax.ppermute(dx, ("section", "dp"), back[t]))
    dyz, = state
    dyz, x_all = lax.optimization_barrier((pack(dyz), x_all))
    kept = keep(owner, anchors, x_all)
    dyz = lax.all_to_all(dyz, "dp", 0, 0, tiled=True).reshape(replicas * rows, share + rank)
    grad_down, grad_up = gradients(at, gt, dyz)
    return kept, grad_down[None], grad_up[None]


def solution(mesh):
    placed = (
        P("section", None, "dp", None, None),
        P("dp", None),
        P("section", None),
        P("section", None, None),
        P("section", None, None),
    )
    return jax.shard_map(
        shards,
        mesh=mesh,
        in_specs=placed,
        out_specs=(
            P("section", "dp", None, None),
            P("section", "dp", None),
            P("section", None, "dp"),
        ),
        check_vma=False,
    )
```
